256 devices in a mesh: pipe: 4 (over y), expert: 16 (over z_lo, x), dp: 4 (over z_hi, core).
Axes of the slice: x: 4, y: 4, z: 8 (z_hi: 2, z_lo: 4; z = z_hi * 4 + z_lo), core: 2. Of those that a mesh axis runs over, the one named last changes fastest.
Arguments:
- fwd_in: bfloat16 [4, 2048, 3584], P('pipe', 'expert'), may hold values from -6 to 6
- fwd_routes: int32 [4, 2048, 2], P('pipe', 'expert'), may hold values from 0 to 15, all different within a row; in each aligned block of 128 rows (0 to 127, 128 to 255, ..., all dimensions but the last counted through in order) at most 20 rows name the same one
- fwd_weights: float32 [4, 2048, 2], P('pipe', 'expert'), may hold values from 0.05 to 0.5
- bwd_saved: bfloat16 [4, 2048, 3584], P('pipe', 'expert'), may hold values from -6 to 6
- bwd_grad: bfloat16 [4, 2048, 3584], P('pipe', 'expert'), may hold values from -6 to 6
- bwd_routes: int32 [4, 2048, 2], P('pipe', 'expert'), may hold values from 0 to 15, all different within a row; in each aligned block of 128 rows (0 to 127, 128 to 255, ..., all dimensions but the last counted through in order) at most 20 rows name the same one
- bwd_weights: float32 [4, 2048, 2], P('pipe', 'expert'), may hold values from 0.05 to 0.5
- expert_gate: bfloat16 [4, 16, 3584, 1024], P('pipe', 'expert', None, 'dp'), may hold values from -0.09375 to 0.09375
- expert_up: bfloat16 [4, 16, 3584, 1024], P('pipe', 'expert', None, 'dp'), may hold values from -0.09375 to 0.09375
- expert_down: bfloat16 [4, 16, 1024, 3584], P('pipe', 'expert', 'dp'), may hold values from -0.1875 to 0.1875
Outputs:
- fwd_out: bfloat16 [4, 2048, 3584], P('pipe', 'expert')
- bwd_out: bfloat16 [4, 2048, 3584], P('pipe', 'expert')
The draws below stay inside these ranges and needn't reach their ends.
Inputs may be any that keep to these rules, and one draw needn't show every extreme that they name: `fwd_routes`: A token names 2 different experts. In every section, the 128 tokens of one index of the expert axis (aligned blocks of rows) name no expert more than 20 times, a bound that some block reaches. `bwd_routes`: A token names 2 different experts. In every section, the 128 tokens of one index of the expert axis (aligned blocks of rows) name no expert more than 20 times, a bound that some block reaches.
All inputs are finite; a program needn't handle non-finite values.
Results may differ from the reference program's by a relative error of at most 0.02.
Values may be sent and summed in bfloat16 or wider, within the bound.
A program may use at most 128 MiB of HBM per device.

```python
import math
import jax
import jax.numpy as jnp
import numpy as np
from jax import lax

D = 3584
FR = 1024
EXPERTS = 16
TOPK = 2
TOK_DEV = 128
CAP = 20
SECTIONS = 4
TOKENS = 2048
N_DP = 4


def block_levels(stream_key, extent, shards, smallest, top_value):
    level = 1.0
    for position, shards_of in shards:
        heights = jax.random.uniform(jax.random.fold_in(jax.random.fold_in(stream_key, 6), position), (shards_of,), jnp.float32, smallest / len(shards), top_value / len(shards))
        level = level * jnp.repeat(jnp.exp(heights), extent[position] // shards_of).reshape((-1,) + (1,) * (len(extent) - 1 - position))
    return level


def shared_out(own_key, own, number, rows, amount, top, bound, slope):
    sequence = jax.random.permutation(own_key, amount)
    heavy_load, usual = portions_of(amount, rows * top, bound, slope, True), portions_of(amount, rows * top, bound, slope, False)
    places = jnp.arange(amount)

    def named(tallies, offset_by):
        used = int((tallies > 0).sum())
        fixed = max(1, used // 4)
        shifted = fixed + (places - fixed + offset_by * (used - fixed)) % max(1, amount - fixed)
        return jnp.zeros((amount,), jnp.int32).at[sequence[jnp.where(places < fixed, places, shifted)]].set(jnp.asarray(tallies, jnp.int32))

    tallies = jnp.where(number % 4 == 0, named(heavy_load, number // 4), named(usual, number - number // 4 - 1))
    mixed = jax.random.permutation(jax.random.fold_in(own, 3), amount)
    giver, taker = mixed[0:amount // 2 * 2:2], mixed[1:amount // 2 * 2:2]
    margin = jnp.minimum(tallies[giver] - 1, bound - tallies[taker]) // 2
    margin = jnp.where((giver == sequence[0]) | (taker == sequence[0]) | (tallies[taker] == 0), 0, jnp.maximum(margin, 0))
    shifted = jax.random.randint(jax.random.fold_in(own, 4), (amount // 2,), 0, 1 << 20) % (margin + 1)
    tallies = tallies.at[giver].add(-shifted).at[taker].add(shifted)
    items = jnp.searchsorted(jnp.cumsum(tallies), jnp.arange(rows * top), side="right").astype(jnp.int32)
    table = items.reshape(top, rows).T
    table = table[jax.random.permutation(jax.random.fold_in(own, 1), rows)]
    offset_by = jax.random.randint(jax.random.fold_in(own, 2), (rows, 1), 0, top)
    return jnp.take_along_axis(table, (jnp.arange(top)[None, :] + offset_by) % top, axis=1)


def portions_of(amount, total, reach, skew, full):
    portions = [(1 << 20) // math.isqrt(grade ** skew) + 1 for grade in range(1, amount + 1)]
    largest = reach if full else min(reach, max(-(-total // amount), total * portions[0] // sum(portions)))
    least = 1 if total - largest >= amount - 1 else 0
    counts, spare = [largest] + [least] * (amount - 1), total - largest - least * (amount - 1)
    while spare > 0:
        movable = [i for i in range(1, amount) if counts[i] < largest] or [i for i in range(1, amount) if counts[i] < reach]
        mass, left = sum([portions[i] for i in movable]), spare
        for i in movable:
            extra = min(reach - counts[i], max(1, left * portions[i] // mass), spare)
            counts[i] = counts[i] + extra
            spare = spare - extra
    return np.array(counts)


def normal_values(stream_key, dims, width, reach, pieces=(), kind=jnp.bfloat16):
    gain = block_levels(stream_key, dims, pieces, -0.22, 0.18) if pieces else 1.0
    result = jax.random.normal(stream_key, dims, jnp.float32) * width * gain
    return jnp.minimum(jnp.maximum(result, -reach), reach).astype(kind)


def setup_inputs(seed: int = 0) -> dict:
    keys = jax.random.split(jax.random.key(seed), 11)
    fwd_in = normal_values(keys[0], (SECTIONS, TOKENS, D), 1.0, 6.0, ((0, 4), (1, 16)))
    fwd_routes_keys = jax.random.split(jax.random.fold_in(keys[1], 1), SECTIONS * TOKENS // TOK_DEV)
    fwd_routes_turns = jax.random.permutation(jax.random.fold_in(keys[1], 3), SECTIONS * TOKENS // TOK_DEV)
    fwd_routes = jax.vmap(lambda own, number: shared_out(jax.random.fold_in(keys[1], 2), own, number, TOK_DEV, EXPERTS, TOPK, CAP, 1))(fwd_routes_keys, fwd_routes_turns).reshape((SECTIONS, TOKENS, TOPK))
    fwd_weights = jnp.clip(jnp.exp(math.log(0.5) - 2.3025851 * jax.random.uniform(keys[2], (SECTIONS, TOKENS, TOPK), jnp.float32) ** block_levels(keys[2], (SECTIONS, TOKENS, TOPK), ((0, 4), (1, 16)), -0.2, 0.2)), 0.05, 0.5)
    bwd_saved = normal_values(keys[3], (SECTIONS, TOKENS, D), 1.0, 6.0, ((0, 4), (1, 16)))
    bwd_grad = normal_values(keys[4], (SECTIONS, TOKENS, D), 1.0, 6.0, ((0, 4), (1, 16)))
    bwd_routes_keys = jax.random.split(jax.random.fold_in(keys[5], 1), SECTIONS * TOKENS // TOK_DEV)
    bwd_routes_turns = jax.random.permutation(jax.random.fold_in(keys[5], 3), SECTIONS * TOKENS // TOK_DEV)
    bwd_routes = jax.vmap(lambda own, number: shared_out(jax.random.fold_in(keys[5], 2), own, number, TOK_DEV, EXPERTS, TOPK, CAP, 1))(bwd_routes_keys, bwd_routes_turns).reshape((SECTIONS, TOKENS, TOPK))
    bwd_weights = jnp.clip(jnp.exp(math.log(0.5) - 2.3025851 * jax.random.uniform(keys[6], (SECTIONS, TOKENS, TOPK), jnp.float32) ** block_levels(keys[6], (SECTIONS, TOKENS, TOPK), ((0, 4), (1, 16)), -0.2, 0.2)), 0.05, 0.5)
    expert_gate = normal_values(keys[7], (SECTIONS, EXPERTS, D, FR), D ** -0.5, 0.09375, ((0, 4), (1, 16), (3, 4)))
    expert_up = normal_values(keys[8], (SECTIONS, EXPERTS, D, FR), D ** -0.5, 0.09375, ((0, 4), (1, 16), (3, 4)))
    expert_down = normal_values(keys[9], (SECTIONS, EXPERTS, FR, D), FR ** -0.5, 0.1875, ((0, 4), (1, 16), (2, 4)))
    return dict(fwd_in=fwd_in, fwd_routes=fwd_routes, fwd_weights=fwd_weights, bwd_saved=bwd_saved, bwd_grad=bwd_grad, bwd_routes=bwd_routes, bwd_weights=bwd_weights, expert_gate=expert_gate, expert_up=expert_up, expert_down=expert_down)


def hidden_of(rows, gate, up):
    gate_pre = jnp.dot(rows, gate, preferred_element_type=jnp.float32)
    up_pre = jnp.dot(rows, up, preferred_element_type=jnp.float32)
    return (jax.nn.silu(gate_pre) * up_pre).astype(jnp.bfloat16)


def blocked_product(hidden, down, blocks):
    count, width_h = hidden.shape
    hid_blocks = hidden.astype(jnp.float32).reshape(count, blocks, width_h // blocks)
    down_blocks = down.astype(jnp.float32).reshape(blocks, width_h // blocks, down.shape[1])
    parts = jnp.einsum("nqh,qhd->qnd", hid_blocks, down_blocks)
    rounded = lax.optimization_barrier(parts.astype(jnp.bfloat16))
    return jnp.sum(rounded.astype(jnp.float32), axis=0)


def grads_of(rows, grads, gate, up, down):
    gate_pre = jnp.dot(rows, gate, preferred_element_type=jnp.float32)
    up_pre = jnp.dot(rows, up, preferred_element_type=jnp.float32)
    back = jnp.dot(grads, down.T, preferred_element_type=jnp.float32)
    sigmoid_gate = jax.nn.sigmoid(gate_pre)
    d_gate = back * up_pre * sigmoid_gate * (1.0 + gate_pre * (1.0 - sigmoid_gate))
    d_up = back * jax.nn.silu(gate_pre)
    return d_gate.astype(jnp.bfloat16), d_up.astype(jnp.bfloat16)


def blocked_back(d_gate, d_up, gate, up, blocks):
    count, width_h = d_gate.shape
    part_h = width_h // blocks
    gate_blocks = gate.astype(jnp.float32).reshape(gate.shape[0], blocks, part_h)
    up_blocks = up.astype(jnp.float32).reshape(up.shape[0], blocks, part_h)
    parts = jnp.einsum("nqh,dqh->qnd", d_gate.astype(jnp.float32).reshape(count, blocks, part_h), gate_blocks)
    parts = parts + jnp.einsum("nqh,dqh->qnd", d_up.astype(jnp.float32).reshape(count, blocks, part_h), up_blocks)
    rounded = lax.optimization_barrier(parts.astype(jnp.bfloat16))
    return jnp.sum(rounded.astype(jnp.float32), axis=0)


def round_trip(values):
    rounded = lax.optimization_barrier(values.astype(jnp.bfloat16))
    return rounded.astype(jnp.float32)


def reference(fwd_in, fwd_routes, fwd_weights, bwd_saved, bwd_grad, bwd_routes, bwd_weights, expert_gate, expert_up, expert_down):
    forward_list = []
    backward_list = []
    indices = jnp.arange(EXPERTS, dtype=jnp.int32)
    for section in range(SECTIONS):
        rows = fwd_in[(section - 1) % SECTIONS]
        routes = fwd_routes[section]
        weights = fwd_weights[section]

        def forward_expert(carry, pack):
            gate, up, down, index = pack
            out = round_trip(blocked_product(hidden_of(rows, gate, up), down, N_DP))
            coef = jnp.sum(jnp.where(routes == index, weights, jnp.float32(0.0)), axis=1)
            return carry + coef[:, None] * out, None

        routed, _ = lax.scan(forward_expert, jnp.zeros(rows.shape, jnp.float32), (expert_gate[section], expert_up[section], expert_down[section], indices))
        forward_list.append(routed.astype(jnp.bfloat16))

        saved = bwd_saved[section]
        grads = bwd_grad[(section + 1) % SECTIONS]
        back_routes = bwd_routes[section]
        back_weights = bwd_weights[section]

        def backward_expert(carry, pack):
            gate, up, down, index = pack
            coef = jnp.sum(jnp.where(back_routes == index, back_weights, jnp.float32(0.0)), axis=1)
            scaled = (coef[:, None] * grads.astype(jnp.float32)).astype(jnp.bfloat16)
            e_gate, e_up = grads_of(saved, scaled, gate, up, down)
            chosen = jnp.sum(jnp.where(back_routes == index, jnp.float32(1.0), jnp.float32(0.0)), axis=1)
            return carry + chosen[:, None] * round_trip(blocked_back(e_gate, e_up, gate, up, N_DP)), None

        routed_back, _ = lax.scan(backward_expert, jnp.zeros(saved.shape, jnp.float32), (expert_gate[section], expert_up[section], expert_down[section], indices))
        backward_list.append(routed_back.astype(jnp.bfloat16))
    return jnp.stack(forward_list), jnp.stack(backward_list)
```

```python
import jax
import jax.numpy as jnp
from jax import lax
from jax.experimental import pallas as pl
from jax.experimental.pallas import tpu as pltpu
from jax.sharding import PartitionSpec as P

MESH = pl.DeviceIdType.MESH
BF16 = jnp.bfloat16
F32 = jnp.float32

BLOCKS = 8
STEP_Z = (0, 0, 1, 1, 2, -2, -1, -1)
CODE = 32
ROWS = BLOCKS * 16
SPARE = BLOCKS * 4
VMEM_LIMIT = 56 * 1024 * 1024


def place():
    pipe = lax.axis_index("pipe")
    expert = lax.axis_index("expert")
    dp = lax.axis_index("dp")
    return pipe, (dp // 2) * 4 + expert // 4, expert % 4, dp % 2


def step_x(k, core):
    return 2 * (k % 2) + (k // 2 + core) % 2


def device_of(pipe, ring, x, core):
    ring = (ring + 16) % 8
    x = (x + 8) % 4
    return ((pipe + 4) % 4, (ring % 4) * 4 + x, (ring // 4) * 2 + core)


def target_of(k, section):
    pipe, ring, x, core = place()
    return device_of(pipe + section, ring + STEP_Z[k], x + step_x(k, core), core)


def source_of(k, section):
    pipe, ring, x, core = place()
    return device_of(pipe + section, ring - STEP_Z[k], x - step_x(k, core), core)


def expert_of_block(b):
    _, ring, x, core = place()
    away = b >> 1
    return (((ring + away) & 3) << 2) + ((x + ((b & 1) << 1) + ((away + core) & 1)) & 3)


def dispatch_kernel(code_x, code_f, code_g, x_ref, f_ref, g_ref, gate, up, down,
                    got_x, got_f, got_g, gate2, up2, down2,
                    send_x, send_f, send_g, send_sem, recv_sem, wsend_sem, wrecv_sem, local_sem):
    pipe, ring, x, core = place()
    sibling = device_of(pipe, ring, x, 1 - core)
    sections = (0, 1, -1)
    quarter = x_ref.shape[1] // 4
    barrier = pltpu.get_barrier_semaphore()

    def greet(who):
        pl.semaphore_signal(barrier, inc=1, device_id=who, device_id_type=MESH)

    greet(sibling)
    for t in range(3):
        for k in range(BLOCKS):
            if t == 0 and k == 0:
                @pl.when(core == 1)
                def _():
                    greet(source_of(0, 0))
            else:
                greet(source_of(k, -sections[t]))

    row = lax.broadcasted_iota(jnp.int32, (ROWS, 1), 0)
    base = expert_of_block(row >> 4) * CODE
    near = base + (row & 15)
    over = base + 16 + (row & 3)
    part = (row >> 2) & 3

    def build(code_ref, rows_ref, send_ref):
        first, second = code_ref[0:1, :], code_ref[1:2, :]
        pick = jnp.where((first == near) | (second == near), 1.0, 0.0).astype(BF16)
        spare = jnp.where((first == over) | (second == over), 1.0, 0.0)
        total = jnp.zeros((ROWS, quarter), F32)
        for q in range(4):
            cols = rows_ref[:, q * quarter:(q + 1) * quarter]
            send_ref[:, q * quarter:(q + 1) * quarter] = jnp.dot(
                pick, cols, preferred_element_type=F32).astype(BF16)
            mine = jnp.where(part == q, spare, 0.0).astype(BF16)
            total = total + jnp.dot(mine, cols, preferred_element_type=F32)
        send_ref[:, 4 * quarter:] = total.astype(BF16)

    def copy(t, k):
        src = (send_x, send_f, send_g)[t]
        dst = (got_x, got_f, got_g)[t]
        return pltpu.make_async_remote_copy(
            src_ref=src.at[pl.ds(16 * k, 16)], dst_ref=dst.at[pl.ds(16 * k, 16)],
            send_sem=send_sem.at[t, k], recv_sem=recv_sem.at[t, k],
            device_id=target_of(k, sections[t]), device_id_type=MESH)

    def weight(i):
        return pltpu.make_async_remote_copy(
            src_ref=(gate, up, down)[i], dst_ref=(gate2, up2, down2)[i],
            send_sem=wsend_sem.at[i], recv_sem=wrecv_sem.at[i],
            device_id=sibling, device_id_type=MESH)

    own = pltpu.make_async_copy(send_x.at[pl.ds(0, 16)], got_x.at[pl.ds(0, 16)], local_sem)

    build(code_x, x_ref, send_x)

    @pl.when(core == 0)
    def _():
        pl.semaphore_wait(barrier, 3 * BLOCKS)

    @pl.when(core == 1)
    def _():
        pl.semaphore_wait(barrier, 3 * BLOCKS + 1)

    for t in range(3):
        if t == 1:
            build(code_f, f_ref, send_f)
        if t == 2:
            build(code_g, g_ref, send_g)
        for k in (4, 5, 2, 3, 6, 7, 1, 0):
            if t == 0 and k == 0:
                @pl.when(core == 0)
                def _():
                    own.start()

                @pl.when(core == 1)
                def _():
                    copy(0, 0).start()
            else:
                copy(t, k).start()
        weight(t).start()
    for t in range(3):
        for k in range(BLOCKS):
            if t == 0 and k == 0:
                @pl.when(core == 0)
                def _():
                    own.wait()

                @pl.when(core == 1)
                def _():
                    copy(0, 0).wait()
            else:
                copy(t, k).wait()
        weight(t).wait()


def dispatch(code_x, code_f, code_g, saved, fwd, grad, gate, up, down):
    width = saved.shape[1]
    packed = jax.ShapeDtypeStruct((ROWS, width + width // 4), BF16)
    vm = pl.BlockSpec(memory_space=pltpu.VMEM)
    hbm = pl.BlockSpec(memory_space=pl.ANY)
    return pl.pallas_call(
        dispatch_kernel,
        name="dispatch",
        out_shape=(packed,) * 3 + tuple(jax.ShapeDtypeStruct(w.shape, w.dtype) for w in (gate, up, down)),
        in_specs=[vm] * 6 + [hbm] * 3,
        out_specs=(hbm,) * 6,
        scratch_shapes=[pltpu.VMEM(packed.shape, BF16)] * 3 + [
            pltpu.SemaphoreType.DMA((3, BLOCKS)), pltpu.SemaphoreType.DMA((3, BLOCKS)),
            pltpu.SemaphoreType.DMA((3,)), pltpu.SemaphoreType.DMA((3,)), pltpu.SemaphoreType.DMA],
        compiler_params=pltpu.CompilerParams(
            collective_id=0, has_side_effects=True, vmem_limit_bytes=VMEM_LIMIT),
    )(code_x, code_f, code_g, saved, fwd, grad, gate, up, down)


def dot_nt(a, b):
    return lax.dot_general(a, b, (((1,), (1,)), ((), ())), preferred_element_type=F32)


def expert_kernel(got_x, got_f, got_g, gate, up, down, gate2, up2, down2, out_f, out_b,
                  left, left_g, pre, back, hid, dgate, dup, spare):
    width = gate.shape[0]
    half = gate.shape[1]
    quarter = width // 4
    rows = ROWS + SPARE
    a = lax.broadcasted_iota(jnp.int32, (SPARE, ROWS), 0)
    b = lax.broadcasted_iota(jnp.int32, (SPARE, ROWS), 1)
    fits = ((a >> 2) == (b >> 4)) & ((a & 3) == (b & 3))
    at = lax.broadcasted_iota(jnp.int32, (ROWS, SPARE), 0)
    bt = lax.broadcasted_iota(jnp.int32, (ROWS, SPARE), 1)
    fits_t = ((bt >> 2) == (at >> 4)) & ((bt & 3) == (at & 3))

    def cols(q):
        return pl.ds(pl.multiple_of(q * quarter, quarter), quarter)

    def unpack(q, _):
        pick = jnp.where(fits & (((b >> 2) & 3) == q), 1.0, 0.0).astype(BF16)
        for src, dst, base in ((got_f, left, 0), (got_x, left, rows), (got_g, left_g, 0)):
            dst[base:base + ROWS, cols(q)] = src[:, cols(q)]
            dst[base + ROWS:base + rows, cols(q)] = jnp.dot(
                pick, src[:, 4 * quarter:], preferred_element_type=F32).astype(BF16)
        return 0

    lax.fori_loop(0, 4, unpack, 0)
    pre[...] = jnp.zeros_like(pre)
    back[...] = jnp.zeros_like(back)

    def first(q, _):
        piece = left[:, cols(q)]
        for i, w in enumerate((gate, gate2, up, up2)):
            pre[:, i * half:(i + 1) * half] += jnp.dot(piece, w[cols(q), :], preferred_element_type=F32)
        piece_g = left_g[:, cols(q)]
        for i, w in enumerate((down, down2)):
            back[:, i * half:(i + 1) * half] += dot_nt(piece_g, w[:, cols(q)])
        return 0

    lax.fori_loop(0, 4, first, 0)
    a_f = pre[:rows, :2 * half]
    hid[...] = (a_f * jax.nn.sigmoid(a_f) * pre[:rows, 2 * half:]).astype(BF16)
    a_b = pre[rows:, :2 * half]
    sig = jax.nn.sigmoid(a_b)
    bk = back[...]
    dgate[...] = (bk * pre[rows:, 2 * half:] * sig * (1.0 + a_b * (1.0 - sig))).astype(BF16)
    dup[...] = (bk * a_b * sig).astype(BF16)
    spare[...] = jnp.zeros_like(spare)

    def second(q, _):
        pack = jnp.where(fits_t & (((at >> 2) & 3) == q), 1.0, 0.0).astype(BF16)
        y = jnp.dot(hid[:, :half], down[:, cols(q)], preferred_element_type=F32)
        y = y + jnp.dot(hid[:, half:], down2[:, cols(q)], preferred_element_type=F32)
        z = dot_nt(dgate[:, :half], gate[cols(q), :])
        z = z + dot_nt(dgate[:, half:], gate2[cols(q), :])
        z = z + dot_nt(dup[:, :half], up[cols(q), :])
        z = z + dot_nt(dup[:, half:], up2[cols(q), :])
        for i, (value, dst) in enumerate(((y, out_f), (z, out_b))):
            value = value.astype(BF16)
            dst[:, cols(q)] = value[:ROWS]
            spare[i] += jnp.dot(pack, value[ROWS:], preferred_element_type=F32)
        return 0

    lax.fori_loop(0, 4, second, 0)
    out_f[:, 4 * quarter:] = spare[0].astype(BF16)
    out_b[:, 4 * quarter:] = spare[1].astype(BF16)


def experts(got_x, got_f, got_g, gate, up, down, gate2, up2, down2):
    width, half = gate.shape
    rows = ROWS + SPARE
    vm = pl.BlockSpec(memory_space=pltpu.VMEM)
    packed = jax.ShapeDtypeStruct(got_x.shape, BF16)
    return pl.pallas_call(
        expert_kernel,
        name="experts",
        out_shape=(packed, packed),
        in_specs=[vm] * 9,
        out_specs=(vm, vm),
        scratch_shapes=[
            pltpu.VMEM((2 * rows, width), BF16), pltpu.VMEM((rows, width), BF16),
            pltpu.VMEM((2 * rows, 4 * half), F32), pltpu.VMEM((rows, 2 * half), F32),
            pltpu.VMEM((rows, 2 * half), BF16), pltpu.VMEM((rows, 2 * half), BF16),
            pltpu.VMEM((rows, 2 * half), BF16), pltpu.VMEM((2, ROWS, width // 4), F32)],
        compiler_params=pltpu.CompilerParams(vmem_limit_bytes=VMEM_LIMIT),
    )(got_x, got_f, got_g, gate, up, down, gate2, up2, down2)


def collect_kernel(code, weights, part_f, part_b, out_f, out_b,
                   back_f, back_b, mine, other, from_other, summed, from_far, final,
                   send_sem, recv_sem, csend, crecv, zsend, zrecv, osend, orecv, local_sem):
    pipe, ring, x, core = place()
    sibling = device_of(pipe, ring, x, 1 - core)
    far = device_of(pipe, ring + 4, x, core)
    half = mine.shape[2]
    quarter = half // 2
    barrier = pltpu.get_barrier_semaphore()

    def greet(who):
        pl.semaphore_signal(barrier, inc=1, device_id=who, device_id_type=MESH)

    greet(sibling)
    greet(far)
    for k in range(1, BLOCKS):
        greet(target_of(k, 0))

    @pl.when(core == 1)
    def _():
        greet(target_of(0, 0))
        pl.semaphore_wait(barrier, BLOCKS + 2)

    @pl.when(core == 0)
    def _():
        pl.semaphore_wait(barrier, BLOCKS + 1)

    def copy(t, k):
        return pltpu.make_async_remote_copy(
            src_ref=(part_f, part_b)[t].at[pl.ds(16 * k, 16)],
            dst_ref=(back_f, back_b)[t].at[pl.ds(16 * k, 16)],
            send_sem=send_sem.at[t, k], recv_sem=recv_sem.at[t, k],
            device_id=source_of(k, 0), device_id_type=MESH)

    def own(t):
        return pltpu.make_async_copy(
            (part_f, part_b)[t].at[pl.ds(0, 16)], (back_f, back_b)[t].at[pl.ds(0, 16)], local_sem.at[t])

    def across(t):
        return pltpu.make_async_remote_copy(
            src_ref=other.at[t], dst_ref=from_other.at[t], send_sem=csend.at[t], recv_sem=crecv.at[t],
            device_id=sibling, device_id_type=MESH)

    def along(t):
        return pltpu.make_async_remote_copy(
            src_ref=summed.at[t], dst_ref=from_far.at[t], send_sem=zsend.at[t], recv_sem=zrecv.at[t],
            device_id=far, device_id_type=MESH)

    my_cols = pl.ds(pl.multiple_of(core * half, half), half)

    def result(t):
        return pltpu.make_async_remote_copy(
            src_ref=final.at[t], dst_ref=(out_f, out_b)[t].at[:, my_cols],
            send_sem=osend.at[t], recv_sem=orecv.at[t], device_id=sibling, device_id_type=MESH)

    def result_here(t):
        return pltpu.make_async_copy(
            final.at[t], (out_f, out_b)[t].at[:, my_cols], local_sem.at[2 + t])

    for t in range(2):
        for k in (4, 5, 2, 3, 6, 7, 1):
            copy(t, k).start()

        @pl.when(core == 0)
        def _():
            own(t).start()

        @pl.when(core == 1)
        def _():
            copy(t, 0).start()

    lane = lax.broadcasted_iota(jnp.int32, (1, ROWS), 1)
    base = expert_of_block(lane >> 4) * CODE
    near = base + (lane & 15)
    over = base + 16 + (lane & 3)
    part = (lane >> 2) & 3

    def split(value):
        high = value.astype(BF16)
        return jnp.concatenate([high, (value - high.astype(F32)).astype(BF16)], axis=0)

    for t in range(2):
        first, second = code[:, 2 * t:2 * t + 1], code[:, 2 * t + 1:2 * t + 2]
        w0, w1 = weights[:, 2 * t:2 * t + 1], weights[:, 2 * t + 1:2 * t + 2]
        pick = split(jnp.where(first == near, w0, 0.0) + jnp.where(second == near, w1, 0.0))
        extra = split(jnp.where(first == over, w0, 0.0) + jnp.where(second == over, w1, 0.0))
        rows_ref = (back_f, back_b)[t]
        for k in range(1, BLOCKS):
            copy(t, k).wait()

        @pl.when(core == 0)
        def _():
            own(t).wait()

        @pl.when(core == 1)
        def _():
            copy(t, 0).wait()

        def chunk(q):
            cols = pl.ds(pl.multiple_of(q * quarter, quarter), quarter)
            here = jnp.where(part == q, extra, jnp.zeros_like(extra))
            both = jnp.dot(pick, rows_ref[:, cols], preferred_element_type=F32)
            both = both + jnp.dot(here, rows_ref[:, 4 * quarter:], preferred_element_type=F32)
            return both[:ROWS] + both[ROWS:]

        for i in range(2):
            other[t, :, i * quarter:(i + 1) * quarter] = chunk(2 * (1 - core) + i).astype(BF16)
        across(t).start()
        for i in range(2):
            mine[t, :, i * quarter:(i + 1) * quarter] = chunk(2 * core + i)
        across(t).wait()
        summed[t] = (mine[t] + from_other[t].astype(F32)).astype(BF16)
        along(t).start()
    for t in range(2):
        along(t).wait()
        final[t] = (summed[t].astype(F32) + from_far[t].astype(F32)).astype(BF16)
        result(t).start()
        result_here(t).start()
    for t in range(2):
        result(t).wait()
        result_here(t).wait()


def collect(code, weights, part_f, part_b, tokens, width):
    vm = pl.BlockSpec(memory_space=pltpu.VMEM)
    hbm = pl.BlockSpec(memory_space=pl.ANY)
    shape = jax.ShapeDtypeStruct((tokens, width), BF16)
    half = (2, tokens, width // 2)
    dma = pltpu.SemaphoreType.DMA
    return pl.pallas_call(
        collect_kernel,
        name="collect",
        out_shape=(shape, shape),
        in_specs=[vm, vm, hbm, hbm],
        out_specs=(hbm, hbm),
        scratch_shapes=[
            pltpu.VMEM(part_f.shape, BF16), pltpu.VMEM(part_f.shape, BF16),
            pltpu.VMEM(half, F32)] + [pltpu.VMEM(half, BF16)] * 5 + [
            dma((2, BLOCKS)), dma((2, BLOCKS)), dma((2,)), dma((2,)), dma((2,)), dma((2,)),
            dma((2,)), dma((2,)), dma((4,))],
        compiler_params=pltpu.CompilerParams(
            collective_id=1, has_side_effects=True, vmem_limit_bytes=VMEM_LIMIT),
    )(code, weights, part_f, part_b)


def slot_codes(routes):
    flat = routes.transpose(0, 2, 1).reshape(routes.shape[0], -1)
    count = flat.shape[1]
    order = jnp.arange(count, dtype=jnp.int32)
    same = (flat[:, :, None] == flat[:, None, :]) & (order[None, :] < order[:, None])[None]
    ranks = jnp.sum(same.astype(jnp.int32), axis=2)
    return (flat * CODE + ranks).reshape(routes.shape[0], routes.shape[2], routes.shape[1])


def body(fwd_in, fwd_routes, fwd_weights, bwd_saved, bwd_grad, bwd_routes, bwd_weights,
         expert_gate, expert_up, expert_down):
    tokens, width = fwd_in.shape[1:]
    codes = slot_codes(jnp.concatenate([fwd_routes, bwd_routes], axis=0))
    code_f = lax.ppermute(codes[0], "pipe", [(i, (i + 3) % 4) for i in range(4)])
    code_g = lax.ppermute(codes[1], "pipe", [(i, (i + 1) % 4) for i in range(4)])
    gate, up, down = expert_gate[0, 0], expert_up[0, 0], expert_down[0, 0]
    got_x, got_f, got_g, gate2, up2, down2 = dispatch(
        codes[1], code_f, code_g, bwd_saved[0], fwd_in[0], bwd_grad[0], gate, up, down)
    part_f, part_b = experts(got_x, got_f, got_g, gate, up, down, gate2, up2, down2)
    code_cols = codes.reshape(4, tokens).T
    weights = jnp.concatenate([fwd_weights[0], bwd_weights[0]], axis=1)
    out_f, out_b = collect(code_cols, weights, part_f, part_b, tokens, width)
    return out_f[None], out_b[None]


def solution(mesh):
    rows = P("pipe", "expert", None)
    wide = P("pipe", "expert", None, "dp")
    return jax.shard_map(
        body,
        mesh=mesh,
        in_specs=(rows,) * 7 + (wide, wide, P("pipe", "expert", "dp", None)),
        out_specs=(rows, rows),
        check_vma=False,
    )
```

```python
import jax
import jax.numpy as jnp
from jax import lax
from jax.experimental import pallas as pl
from jax.experimental.pallas import tpu as pltpu
from jax.sharding import PartitionSpec as P

MESH = pl.DeviceIdType.MESH
BF16 = jnp.bfloat16
F32 = jnp.float32

BLOCKS = 8
STEP_Z = (0, 0, 1, 1, 2, -2, -1, -1)
FAR_FIRST = (4, 5, 2, 3, 6, 7, 1, 0)
CODE = 32
ROWS = BLOCKS * 16
SPARE = BLOCKS * 4
ALL = ROWS + SPARE
VMEM_LIMIT = 56 * 1024 * 1024
SECTION = (0, -1, 1)
B, F = 0, 1


def place():
    pipe = lax.axis_index("pipe")
    expert = lax.axis_index("expert")
    dp = lax.axis_index("dp")
    return pipe, (dp // 2) * 4 + expert // 4, expert % 4, dp % 2


def step_x(k, core):
    return 2 * (k % 2) + (k // 2 + core) % 2


def device_of(pipe, ring, x, core):
    ring = (ring + 16) % 8
    x = (x + 8) % 4
    return ((pipe + 4) % 4, (ring % 4) * 4 + x, (ring // 4) * 2 + core)


def target_of(k, section):
    pipe, ring, x, core = place()
    return device_of(pipe + section, ring + STEP_Z[k], x + step_x(k, core), core)


def source_of(k, section):
    pipe, ring, x, core = place()
    return device_of(pipe + section, ring - STEP_Z[k], x - step_x(k, core), core)


def expert_of_block(b):
    _, ring, x, core = place()
    away = b >> 1
    return (((ring + away) & 3) << 2) + ((x + ((b & 1) << 1) + ((away + core) & 1)) & 3)


def dot(a, b):
    return jnp.dot(a, b, preferred_element_type=F32)


def dot_nt(a, b):
    return lax.dot_general(a, b, (((1,), (1,)), ((), ())), preferred_element_type=F32)


def iota(shape, dim):
    return lax.broadcasted_iota(jnp.int32, shape, dim)


def kernel(routes_f, routes_b, weights_f, weights_b, x_ref, g_ref, f_ref, gate, up, down,
           out_f, out_b,
           send, got, left, tall, tall_down, pre, back, hid, dgate, dup, spare,
           part, home, mine, other, from_other, summed, from_far, final, codes,
           send_sem, recv_sem, wlocal, wsend, wrecv, codesend, coderecv,
           rsend, rrecv, csend, crecv, zsend, zrecv, osend, orecv, local_sem):
    pipe, ring, x, core = place()
    sibling = device_of(pipe, ring, x, 1 - core)
    far = device_of(pipe, ring + 4, x, core)
    after = device_of(pipe + 1, ring, x, core)
    before = device_of(pipe - 1, ring, x, core)
    tokens, width = x_ref.shape
    quarter = width // 4
    half = width // 2
    hidden = gate.shape[1]
    barrier = pltpu.get_barrier_semaphore()

    def greet(who):
        pl.semaphore_signal(barrier, inc=1, device_id=who, device_id_type=MESH)

    def unless_self(k, does, instead=None):
        if k:
            does()
            return
        pl.when(core == 1)(does)
        if instead is not None:
            pl.when(core == 0)(instead)

    for who in (sibling, far, after, before):
        greet(who)
    for k in range(BLOCKS):
        unless_self(k, lambda: greet(source_of(k, 0)))
        unless_self(k, lambda: greet(target_of(k, 0)))
        greet(source_of(k, -SECTION[1]))
        greet(source_of(k, -SECTION[2]))

    def here(i):
        src = (gate, up, down)[i]
        dst = tall_down.at[core] if i == 2 else tall.at[core, i]
        return pltpu.make_async_copy(src, dst, wlocal.at[i])

    def weight(i):
        src = (gate, up, down)[i]
        dst = tall_down.at[core] if i == 2 else tall.at[core, i]
        return pltpu.make_async_remote_copy(
            src_ref=src, dst_ref=dst, send_sem=wsend.at[i], recv_sem=wrecv.at[i],
            device_id=sibling, device_id_type=MESH)

    for i in range(3):
        here(i).start()

    sub, lane = iota((tokens, tokens), 0), iota((tokens, tokens), 1)

    def as_row(col):
        return jnp.sum(jnp.where(sub == lane, col, 0.0), axis=0, keepdims=True)

    def as_col(row):
        return jnp.sum(jnp.where(sub == lane, row, 0.0), axis=1, keepdims=True)

    def count(flags):
        return jnp.sum(jnp.where(flags, 1.0, 0.0), axis=0, keepdims=True)

    def code_rows(routes):
        c0, c1 = routes[:, 0:1].astype(F32), routes[:, 1:2].astype(F32)
        r0, r1 = as_row(c0), as_row(c1)
        rank0 = count((c0 == r0) & (sub < lane))
        rank1 = count(c0 == r1) + count((c1 == r1) & (sub < lane))
        return r0 * CODE + rank0, r1 * CODE + rank1

    cols = []
    codes[0:2] = jnp.zeros_like(codes[0:2])
    for i, routes in enumerate((routes_b, routes_f)):
        first, second = code_rows(routes)
        codes[i, 0:1, :] = first
        codes[i, 1:2, :] = second
        cols.append((as_col(first), as_col(second)))

    def swap(i):
        return pltpu.make_async_remote_copy(
            src_ref=codes.at[i], dst_ref=codes.at[2 + i], send_sem=codesend.at[i], recv_sem=coderecv.at[i],
            device_id=(after, before)[i], device_id_type=MESH)

    def blocks_of(index):
        expert = expert_of_block(index >> 4) * CODE
        return (expert + (index & 15)).astype(F32), (expert + 16 + (index & 3)).astype(F32), (index >> 2) & 3

    near_col, over_col, part_col = blocks_of(iota((ROWS, 1), 0))

    def build(t, code, rows_ref):
        first, second = codes[code, 0:1, :], codes[code, 1:2, :]
        pick = jnp.where((first == near_col) | (second == near_col), 1.0, 0.0).astype(BF16)
        extra = jnp.where((first == over_col) | (second == over_col), 1.0, 0.0)
        total = jnp.zeros((ROWS, quarter), F32)
        for q in range(4):
            piece = rows_ref[:, q * quarter:(q + 1) * quarter]
            send[t, :, q * quarter:(q + 1) * quarter] = dot(pick, piece).astype(BF16)
            total = total + dot(jnp.where(part_col == q, extra, 0.0).astype(BF16), piece)
        send[t, :, width:] = total.astype(BF16)

    def outward(t, k):
        block = pl.ds(16 * k, 16)
        return pltpu.make_async_remote_copy(
            src_ref=send.at[t, block], dst_ref=got.at[t, block],
            send_sem=send_sem.at[t, k], recv_sem=recv_sem.at[t, k],
            device_id=target_of(k, SECTION[t]), device_id_type=MESH)

    def own_outward():
        return pltpu.make_async_copy(send.at[0, pl.ds(0, 16)], got.at[0, pl.ds(0, 16)], local_sem.at[0])

    def send_out(t):
        for k in FAR_FIRST:
            if t == 0:
                unless_self(k, lambda: outward(t, k).start(), lambda: own_outward().start())
            else:
                outward(t, k).start()

    def wait_out(t):
        for k in FAR_FIRST:
            if t == 0:
                unless_self(k, lambda: outward(t, k).wait(), lambda: own_outward().wait())
            else:
                outward(t, k).wait()

    build(0, 0, x_ref)
    pl.semaphore_wait(barrier, 4 * BLOCKS + 2 + 2 * core)
    swap(0).start()
    swap(1).start()
    send_out(0)
    for i in range(3):
        weight(i).start()
    swap(0).wait()
    build(1, 2, g_ref)
    send_out(1)
    swap(1).wait()
    build(2, 3, f_ref)
    send_out(2)

    a, b = iota((SPARE, ROWS), 0), iota((SPARE, ROWS), 1)
    fits = ((a >> 2) == (b >> 4)) & ((a & 3) == (b & 3))
    at, bt = iota((ROWS, SPARE), 0), iota((ROWS, SPARE), 1)
    fits_t = ((bt >> 2) == (at >> 4)) & ((bt & 3) == (at & 3))

    def columns(q):
        return pl.ds(pl.multiple_of(q * quarter, quarter), quarter)

    def unpack(t):
        def step(q, _):
            pick = jnp.where(fits & (((b >> 2) & 3) == q), 1.0, 0.0).astype(BF16)
            left[:ROWS, columns(q)] = got[t, :, columns(q)]
            left[ROWS:, columns(q)] = dot(pick, got[t, :, width:]).astype(BF16)
            return 0
        lax.fori_loop(0, 4, step, 0)

    def first_layer():
        pre[...] = jnp.zeros_like(pre)

        def step(q, _):
            piece = left[:, columns(q)]
            for c in range(2):
                for i in range(2):
                    lo = (2 * i + c) * hidden
                    pre[:, lo:lo + hidden] += dot(piece, tall[c, i, columns(q), :])
            return 0
        lax.fori_loop(0, 4, step, 0)

    def back_layer():
        back[...] = jnp.zeros_like(back)

        def step(q, _):
            piece = left[:, columns(q)]
            for c in range(2):
                back[:, c * hidden:(c + 1) * hidden] += dot_nt(piece, tall_down[c, :, columns(q)])
            return 0
        lax.fori_loop(0, 4, step, 0)

    def second_layer(r, product):
        spare[...] = jnp.zeros_like(spare)

        def step(q, _):
            pack = jnp.where(fits_t & (((at >> 2) & 3) == q), 1.0, 0.0).astype(BF16)
            value = product(q).astype(BF16)
            part[r, :, columns(q)] = value[:ROWS]
            spare[...] += dot(pack, value[ROWS:])
            return 0
        lax.fori_loop(0, 4, step, 0)
        part[r, :, width:] = spare[...].astype(BF16)

    def forward_product(q):
        return (dot(hid[:, :hidden], tall_down[0, :, columns(q)])
                + dot(hid[:, hidden:], tall_down[1, :, columns(q)]))

    def backward_product(q):
        total = dot_nt(dgate[:, :hidden], tall[0, 0, columns(q), :])
        total = total + dot_nt(dgate[:, hidden:], tall[1, 0, columns(q), :])
        total = total + dot_nt(dup[:, :hidden], tall[0, 1, columns(q), :])
        return total + dot_nt(dup[:, hidden:], tall[1, 1, columns(q), :])

    def homeward(r, k):
        block = pl.ds(16 * k, 16)
        return pltpu.make_async_remote_copy(
            src_ref=part.at[r, block], dst_ref=home.at[r, block],
            send_sem=rsend.at[r, k], recv_sem=rrecv.at[r, k],
            device_id=source_of(k, 0), device_id_type=MESH)

    def own_homeward(r):
        return pltpu.make_async_copy(part.at[r, pl.ds(0, 16)], home.at[r, pl.ds(0, 16)], local_sem.at[1 + r])

    def send_home(r):
        for k in FAR_FIRST:
            unless_self(k, lambda: homeward(r, k).start(), lambda: own_homeward(r).start())

    def wait_home(r):
        for k in FAR_FIRST:
            unless_self(k, lambda: homeward(r, k).wait(), lambda: own_homeward(r).wait())

    for i in range(3):
        here(i).wait()
        weight(i).wait()
    wait_out(0)
    unpack(0)
    first_layer()
    wait_out(1)
    unpack(1)
    back_layer()
    pre_a = pre[:, :2 * hidden]
    sig = jax.nn.sigmoid(pre_a)
    bk = back[...]
    dgate[...] = (bk * pre[:, 2 * hidden:] * sig * (1.0 + pre_a * (1.0 - sig))).astype(BF16)
    dup[...] = (bk * pre_a * sig).astype(BF16)
    second_layer(B, backward_product)
    send_home(B)
    wait_out(2)
    unpack(2)
    first_layer()
    pre_a = pre[:, :2 * hidden]
    hid[...] = (pre_a * jax.nn.sigmoid(pre_a) * pre[:, 2 * hidden:]).astype(BF16)
    second_layer(F, forward_product)
    send_home(F)

    near_row, over_row, part_row = blocks_of(iota((1, ROWS), 1))
    my_cols = pl.ds(pl.multiple_of(core * half, half), half)

    def split(value):
        high = value.astype(BF16)
        return jnp.concatenate([high, (value - high.astype(F32)).astype(BF16)], axis=0)

    def across(r):
        return pltpu.make_async_remote_copy(
            src_ref=other.at[r], dst_ref=from_other.at[r], send_sem=csend.at[r], recv_sem=crecv.at[r],
            device_id=sibling, device_id_type=MESH)

    def along(r):
        return pltpu.make_async_remote_copy(
            src_ref=summed.at[r], dst_ref=from_far.at[r], send_sem=zsend.at[r], recv_sem=zrecv.at[r],
            device_id=far, device_id_type=MESH)

    def result(r):
        return pltpu.make_async_remote_copy(
            src_ref=final.at[r], dst_ref=(out_b, out_f)[r].at[:, my_cols],
            send_sem=osend.at[r], recv_sem=orecv.at[r], device_id=sibling, device_id_type=MESH)

    def result_here(r):
        return pltpu.make_async_copy(final.at[r], (out_b, out_f)[r].at[:, my_cols], local_sem.at[3 + r])

    for r in (B, F):
        weights = (weights_b, weights_f)[r]
        w0, w1 = weights[:, 0:1], weights[:, 1:2]
        first, second = cols[r]
        pick = split(jnp.where(first == near_row, w0, 0.0) + jnp.where(second == near_row, w1, 0.0))
        extra = split(jnp.where(first == over_row, w0, 0.0) + jnp.where(second == over_row, w1, 0.0))
        wait_home(r)

        def chunk(q):
            mask = jnp.where(part_row == q, extra, jnp.zeros_like(extra))
            both = dot(pick, home[r, :, columns(q)]) + dot(mask, home[r, :, width:])
            return both[:tokens] + both[tokens:]

        for i in range(2):
            other[r, :, i * quarter:(i + 1) * quarter] = chunk(2 * (1 - core) + i).astype(BF16)
        across(r).start()
        for i in range(2):
            mine[:, i * quarter:(i + 1) * quarter] = chunk(2 * core + i)
        across(r).wait()
        summed[r] = (mine[...] + from_other[r].astype(F32)).astype(BF16)
        along(r).start()
    for r in (B, F):
        along(r).wait()
        final[r] = (summed[r].astype(F32) + from_far[r].astype(F32)).astype(BF16)
        result(r).start()
        result_here(r).start()
    for r in (B, F):
        result(r).wait()
        result_here(r).wait()


def body(fwd_in, fwd_routes, fwd_weights, bwd_saved, bwd_grad, bwd_routes, bwd_weights,
         expert_gate, expert_up, expert_down):
    tokens, width = fwd_in.shape[1:]
    hidden = expert_gate.shape[3]
    packed = (ROWS, width + width // 4)
    half = (2, tokens, width // 2)
    vm = pl.BlockSpec(memory_space=pltpu.VMEM)
    hbm = pl.BlockSpec(memory_space=pl.ANY)
    dma = pltpu.SemaphoreType.DMA
    shape = jax.ShapeDtypeStruct((tokens, width), BF16)
    out_f, out_b = pl.pallas_call(
        kernel,
        name="experts",
        out_shape=(shape, shape),
        in_specs=[vm] * 7 + [hbm] * 3,
        out_specs=(hbm, hbm),
        scratch_shapes=[
            pltpu.VMEM((3,) + packed, BF16), pltpu.VMEM((3,) + packed, BF16),
            pltpu.VMEM((ALL, width), BF16),
            pltpu.VMEM((2, 2, width, hidden), BF16), pltpu.VMEM((2, hidden, width), BF16),
            pltpu.VMEM((ALL, 4 * hidden), F32), pltpu.VMEM((ALL, 2 * hidden), F32),
            pltpu.VMEM((ALL, 2 * hidden), BF16), pltpu.VMEM((ALL, 2 * hidden), BF16),
            pltpu.VMEM((ALL, 2 * hidden), BF16),
            pltpu.VMEM((ROWS, width // 4), F32),
            pltpu.VMEM((2,) + packed, BF16), pltpu.VMEM((2,) + packed, BF16),
            pltpu.VMEM(half[1:], F32)] + [pltpu.VMEM(half, BF16)] * 5 + [
            pltpu.VMEM((4, 8, 128), F32),
            dma((3, BLOCKS)), dma((3, BLOCKS)), dma((3,)), dma((3,)), dma((3,)), dma((2,)), dma((2,)),
            dma((2, BLOCKS)), dma((2, BLOCKS)), dma((2,)), dma((2,)), dma((2,)), dma((2,)),
            dma((2,)), dma((2,)), dma((5,))],
        compiler_params=pltpu.CompilerParams(
            collective_id=0, has_side_effects=True, vmem_limit_bytes=VMEM_LIMIT),
    )(fwd_routes[0], bwd_routes[0], fwd_weights[0], bwd_weights[0], bwd_saved[0], bwd_grad[0], fwd_in[0],
      expert_gate[0, 0], expert_up[0, 0], expert_down[0, 0])
    return out_f[None], out_b[None]


def solution(mesh):
    rows = P("pipe", "expert", None)
    wide = P("pipe", "expert", None, "dp")
    return jax.shard_map(
        body,
        mesh=mesh,
        in_specs=(rows,) * 7 + (wide, wide, P("pipe", "expert", "dp", None)),
        out_specs=(rows, rows),
        check_vma=False,
    )
```

```python
import jax
import jax.numpy as jnp
from jax import lax
from jax.experimental import pallas as pl
from jax.experimental.pallas import tpu as pltpu
from jax.sharding import PartitionSpec as P

MESH = pl.DeviceIdType.MESH
BF16 = jnp.bfloat16
F32 = jnp.float32

BLOCKS = 8
STEP_Z = (0, 0, 1, 1, 2, -2, -1, -1)
FAR_FIRST = (4, 5, 2, 3, 6, 7, 1, 0)
CODE = 32
ROWS = BLOCKS * 16
SPARE = BLOCKS * 4
ALL = ROWS + SPARE
VMEM_LIMIT = 56 * 1024 * 1024
SECTION = (0, -1, 1)
GROUP = 512
FOLD = GROUP // 4
WIDE = GROUP + FOLD
CHUNKS = 2
B, F = 0, 1


def place():
    pipe = lax.axis_index("pipe")
    expert = lax.axis_index("expert")
    dp = lax.axis_index("dp")
    return pipe, (dp // 2) * 4 + expert // 4, expert % 4, dp % 2


def step_x(k, core):
    return 2 * (k % 2) + (k // 2 + core) % 2


def device_of(pipe, ring, x, core):
    ring = (ring + 16) % 8
    x = (x + 8) % 4
    return ((pipe + 4) % 4, (ring % 4) * 4 + x, (ring // 4) * 2 + core)


def target_of(k):
    pipe, ring, x, core = place()
    return device_of(pipe, ring + STEP_Z[k], x + step_x(k, core), core)


def source_of(k):
    pipe, ring, x, core = place()
    return device_of(pipe, ring - STEP_Z[k], x - step_x(k, core), core)


def expert_of_block(b):
    _, ring, x, core = place()
    away = b >> 1
    return (((ring + away) & 3) << 2) + ((x + ((b & 1) << 1) + ((away + core) & 1)) & 3)


def dot(a, b):
    return jnp.dot(a, b, preferred_element_type=F32)


def dot_nt(a, b):
    return lax.dot_general(a, b, (((1,), (1,)), ((), ())), preferred_element_type=F32)


def iota(shape, dim):
    return lax.broadcasted_iota(jnp.int32, shape, dim)


def kernel(routes_f, routes_b, weights_f, weights_b, x_ref, g_ref, f_ref, gate, up, down,
           out_f, out_b,
           send, got, left, tall, tall_down, pre, back, hid, dgate, dup,
           part, home, comb, mine, other, from_other, summed, from_far, final, moved,
           send_sem, recv_sem, wlocal, wsend, wrecv, shift_send, shift_recv, pass_send, pass_recv,
           rsend, rrecv, rlocal, csend, crecv, zsend, zrecv, osend, orecv, olocal, local_sem):
    pipe, ring, x, core = place()
    sibling = device_of(pipe, ring, x, 1 - core)
    far = device_of(pipe, ring + 4, x, core)
    after = device_of(pipe + 1, ring, x, core)
    before = device_of(pipe - 1, ring, x, core)
    tokens, width = x_ref.shape
    quarter = width // 4
    groups = width // GROUP
    cuts = [groups * i // CHUNKS for i in range(CHUNKS + 1)]
    hidden = gate.shape[1]
    barrier = pltpu.get_barrier_semaphore()

    def greet(who):
        pl.semaphore_signal(barrier, inc=1, device_id=who, device_id_type=MESH)

    def unless_self(k, does, instead=None):
        if k:
            does()
            return
        pl.when(core == 1)(does)
        if instead is not None:
            pl.when(core == 0)(instead)

    for who in (sibling, far, after, before):
        greet(who)
    for k in range(BLOCKS):
        unless_self(k, lambda: greet(source_of(k)))
        unless_self(k, lambda: greet(target_of(k)))

    def here(i):
        src = (gate, up, down)[i]
        dst = tall_down.at[core] if i == 2 else tall.at[core, i]
        return pltpu.make_async_copy(src, dst, wlocal.at[i])

    def weight(i):
        src = (gate, up, down)[i]
        dst = tall_down.at[core] if i == 2 else tall.at[core, i]
        return pltpu.make_async_remote_copy(
            src_ref=src, dst_ref=dst, send_sem=wsend.at[i], recv_sem=wrecv.at[i],
            device_id=sibling, device_id_type=MESH)

    for i in range(3):
        here(i).start()

    sub, lane = iota((tokens, tokens), 0), iota((tokens, tokens), 1)

    def as_col(row):
        return jnp.sum(jnp.where(sub == lane, row, 0.0), axis=1, keepdims=True)

    def count(flags):
        return jnp.sum(jnp.where(flags, 1.0, 0.0), axis=0, keepdims=True)

    def code_rows(routes):
        r0, r1 = routes[0:1, :].astype(F32), routes[1:2, :].astype(F32)
        c0, c1 = as_col(r0), as_col(r1)
        rank0 = count((c0 == r0) & (sub < lane))
        rank1 = count(c0 == r1) + count((c1 == r1) & (sub < lane))
        return r0 * CODE + rank0, r1 * CODE + rank1

    half = tokens // 2
    my_half = pl.ds(pl.multiple_of(core * half, half), half)

    def shift(t):
        return pltpu.make_async_remote_copy(
            src_ref=(None, g_ref, f_ref)[t].at[my_half], dst_ref=moved.at[t - 1, my_half],
            send_sem=shift_send.at[t - 1], recv_sem=shift_recv.at[t - 1],
            device_id=(None, before, after)[t], device_id_type=MESH)

    def pass_on(t):
        return pltpu.make_async_remote_copy(
            src_ref=moved.at[t - 1, my_half], dst_ref=moved.at[t - 1, my_half],
            send_sem=pass_send.at[t - 1], recv_sem=pass_recv.at[t - 1],
            device_id=sibling, device_id_type=MESH)

    def blocks_of(index):
        expert = expert_of_block(index >> 4) * CODE
        return (expert + (index & 15)).astype(F32), (expert + 16 + (index & 3)).astype(F32), (index >> 2) & 3

    near_col, over_col, part_col = blocks_of(iota((ROWS, 1), 0))

    def build(t, code, rows_ref):
        first, second = code
        pick = jnp.where((first == near_col) | (second == near_col), 1.0, 0.0).astype(BF16)
        extra = jnp.where((first == over_col) | (second == over_col), 1.0, 0.0)
        total = jnp.zeros((ROWS, quarter), F32)
        for q in range(4):
            piece = rows_ref[:, q * quarter:(q + 1) * quarter]
            send[t, :, q * quarter:(q + 1) * quarter] = dot(pick, piece).astype(BF16)
            total = total + dot(jnp.where(part_col == q, extra, 0.0).astype(BF16), piece)
        send[t, :, width:] = total.astype(BF16)

    def outward(t, k):
        block = pl.ds(16 * k, 16)
        return pltpu.make_async_remote_copy(
            src_ref=send.at[t, block], dst_ref=got.at[t, block],
            send_sem=send_sem.at[t, k], recv_sem=recv_sem.at[t, k],
            device_id=target_of(k), device_id_type=MESH)

    def own_outward(t):
        return pltpu.make_async_copy(send.at[t, pl.ds(0, 16)], got.at[t, pl.ds(0, 16)], local_sem.at[t])

    def send_out(t):
        for k in FAR_FIRST:
            unless_self(k, lambda: outward(t, k).start(), lambda: own_outward(t).start())

    def wait_out(t):
        for k in FAR_FIRST:
            unless_self(k, lambda: outward(t, k).wait(), lambda: own_outward(t).wait())

    pl.semaphore_wait(barrier, 2 * BLOCKS + 2 + 2 * core)
    shift(1).start()
    shift(2).start()
    for i in range(3):
        weight(i).start()
    codes = [code_rows(routes) for routes in (routes_b, routes_f)]
    build(0, codes[B], x_ref)
    send_out(0)
    for t in (1, 2):
        shift(t).wait()
        pass_on(t).start()
    for t in (1, 2):
        pass_on(t).wait()
        build(t, codes[t - 1], moved.at[t - 1])
        send_out(t)

    near_row, over_row, part_row = blocks_of(iota((1, ROWS), 1))
    for r, weights in enumerate((weights_b, weights_f)):
        w0, w1 = as_col(weights[0:1, :]), as_col(weights[1:2, :])
        first, second = as_col(codes[r][0]), as_col(codes[r][1])
        pick = jnp.where(first == near_row, w0, 0.0) + jnp.where(second == near_row, w1, 0.0)
        extra = jnp.where(first == over_row, w0, 0.0) + jnp.where(second == over_row, w1, 0.0)
        for j in range(5):
            value = pick if j == 0 else jnp.where(part_row == j - 1, extra, 0.0)
            high = value.astype(BF16)
            comb[r, j, :tokens, :] = high
            comb[r, j, tokens:, :] = (value - high.astype(F32)).astype(BF16)

    a, b = iota((SPARE, ROWS), 0), iota((SPARE, ROWS), 1)
    fits = ((a >> 2) == (b >> 4)) & ((a & 3) == (b & 3))
    at, bt = iota((ROWS, SPARE), 0), iota((ROWS, SPARE), 1)
    fits_t = ((bt >> 2) == (at >> 4)) & ((bt & 3) == (at & 3))

    def columns(q):
        return pl.ds(pl.multiple_of(q * quarter, quarter), quarter)

    def unpack(t):
        def step(q, _):
            pick = jnp.where(fits & (((b >> 2) & 3) == q), 1.0, 0.0).astype(BF16)
            left[:ROWS, columns(q)] = got[t, :, columns(q)]
            left[ROWS:, columns(q)] = dot(pick, got[t, :, width:]).astype(BF16)
            return 0
        lax.fori_loop(0, 4, step, 0)

    def first_layer():
        pre[...] = jnp.zeros_like(pre)

        def step(q, _):
            piece = left[:, columns(q)]
            for c in range(2):
                for i in range(2):
                    lo = (2 * i + c) * hidden
                    pre[:, lo:lo + hidden] += dot(piece, tall[c, i, columns(q), :])
            return 0
        lax.fori_loop(0, 4, step, 0)

    def back_layer():
        back[...] = jnp.zeros_like(back)

        def step(q, _):
            piece = left[:, columns(q)]
            for c in range(2):
                back[:, c * hidden:(c + 1) * hidden] += dot_nt(piece, tall_down[c, :, columns(q)])
            return 0
        lax.fori_loop(0, 4, step, 0)

    packs = [jnp.where(fits_t & (((at >> 2) & 3) == q), 1.0, 0.0).astype(BF16) for q in range(4)]

    def group_cols(g, start=0, size=GROUP, pitch=GROUP):
        return pl.ds(pl.multiple_of(g * pitch + start, FOLD), size)

    def second_layer(r, n, product):
        def step(g, _):
            value = product(group_cols(g)).astype(BF16)
            part[r, :, group_cols(g, 0, GROUP, WIDE)] = value[:ROWS]
            rest = value[ROWS:]
            folded = dot(packs[0], rest[:, :FOLD])
            for q in range(1, 4):
                folded = folded + dot(packs[q], rest[:, q * FOLD:(q + 1) * FOLD])
            part[r, :, group_cols(g, GROUP, FOLD, WIDE)] = folded.astype(BF16)
            return 0
        lax.fori_loop(cuts[n], cuts[n + 1], step, 0)

    def forward_product(span):
        return dot(hid[:, :hidden], tall_down[0, :, span]) + dot(hid[:, hidden:], tall_down[1, :, span])

    def backward_product(span):
        total = dot_nt(dgate[:, :hidden], tall[0, 0, span, :])
        total = total + dot_nt(dgate[:, hidden:], tall[1, 0, span, :])
        total = total + dot_nt(dup[:, :hidden], tall[0, 1, span, :])
        return total + dot_nt(dup[:, hidden:], tall[1, 1, span, :])

    def packed_cols(n):
        return pl.ds(cuts[n] * WIDE, (cuts[n + 1] - cuts[n]) * WIDE)

    def homeward(r, n, k):
        block = pl.ds(16 * k, 16)
        return pltpu.make_async_remote_copy(
            src_ref=part.at[r, block, packed_cols(n)], dst_ref=home.at[r, block, packed_cols(n)],
            send_sem=rsend.at[r, n, k], recv_sem=rrecv.at[r, n, k],
            device_id=source_of(k), device_id_type=MESH)

    def own_homeward(r, n):
        block = pl.ds(0, 16)
        return pltpu.make_async_copy(
            part.at[r, block, packed_cols(n)], home.at[r, block, packed_cols(n)], rlocal.at[r, n])

    def send_home(r, n):
        for k in FAR_FIRST:
            unless_self(k, lambda: homeward(r, n, k).start(), lambda: own_homeward(r, n).start())

    def wait_home(r, n):
        for k in FAR_FIRST:
            unless_self(k, lambda: homeward(r, n, k).wait(), lambda: own_homeward(r, n).wait())

    for i in range(3):
        here(i).wait()
        weight(i).wait()
    wait_out(0)
    unpack(0)
    first_layer()
    wait_out(1)
    unpack(1)
    back_layer()
    pre_a = pre[:, :2 * hidden]
    sig = jax.nn.sigmoid(pre_a)
    bk = back[...]
    dgate[...] = (bk * pre[:, 2 * hidden:] * sig * (1.0 + pre_a * (1.0 - sig))).astype(BF16)
    dup[...] = (bk * pre_a * sig).astype(BF16)
    for n in range(CHUNKS):
        second_layer(B, n, backward_product)
        send_home(B, n)
    wait_out(2)
    unpack(2)
    first_layer()
    pre_a = pre[:, :2 * hidden]
    hid[...] = (pre_a * jax.nn.sigmoid(pre_a) * pre[:, 2 * hidden:]).astype(BF16)
    for n in range(CHUNKS):
        second_layer(F, n, forward_product)
        send_home(F, n)

    def span_of(n):
        return pl.ds(cuts[n] * GROUP, (cuts[n + 1] - cuts[n]) * GROUP)

    def half_of(which):
        return pl.multiple_of(which * half, half)

    def across(r, n):
        return pltpu.make_async_remote_copy(
            src_ref=other.at[r, :, span_of(n)], dst_ref=from_other.at[r, :, span_of(n)],
            send_sem=csend.at[r, n], recv_sem=crecv.at[r, n], device_id=sibling, device_id_type=MESH)

    def along(r, n):
        return pltpu.make_async_remote_copy(
            src_ref=summed.at[r, :, span_of(n)], dst_ref=from_far.at[r, :, span_of(n)],
            send_sem=zsend.at[r, n], recv_sem=zrecv.at[r, n], device_id=far, device_id_type=MESH)

    def my_result(r, n):
        return (out_b, out_f)[r].at[pl.ds(half_of(core), half), span_of(n)]

    def result(r, n):
        return pltpu.make_async_remote_copy(
            src_ref=final.at[r, :, span_of(n)], dst_ref=my_result(r, n),
            send_sem=osend.at[r, n], recv_sem=orecv.at[r, n], device_id=sibling, device_id_type=MESH)

    def result_here(r, n):
        return pltpu.make_async_copy(final.at[r, :, span_of(n)], my_result(r, n), olocal.at[r, n])

    def combine(r, n, which, dst):
        def rows_of(j):
            start = half_of(which)
            return jnp.concatenate([comb[r, j, pl.ds(start, half), :],
                                    comb[r, j, pl.ds(tokens + start, half), :]], axis=0)
        mats = [rows_of(j) for j in range(5)]

        def step(g, _):
            folded = home[r, :, group_cols(g, GROUP, FOLD, WIDE)]
            both = dot(mats[0], home[r, :, group_cols(g, 0, GROUP, WIDE)])
            both = both + jnp.concatenate([dot(m, folded) for m in mats[1:]], axis=1)
            dst[r, :, group_cols(g)] = (both[:half] + both[half:]).astype(dst.dtype)
            return 0
        lax.fori_loop(cuts[n], cuts[n + 1], step, 0)

    def gather(r):
        for n in range(CHUNKS):
            wait_home(r, n)
            combine(r, n, 1 - core, other)
            across(r, n).start()
            combine(r, n, core, mine)
            span = span_of(n)
            across(r, n).wait()
            summed[r, :, span] = (mine[r, :, span] + from_other[r, :, span].astype(F32)).astype(BF16)
            along(r, n).start()

    def finish(r):
        for n in range(CHUNKS):
            span = span_of(n)
            along(r, n).wait()
            final[r, :, span] = (summed[r, :, span].astype(F32) + from_far[r, :, span].astype(F32)).astype(BF16)
            result(r, n).start()
            result_here(r, n).start()

    gather(B)
    gather(F)
    finish(B)
    finish(F)
    for r in (B, F):
        for n in range(CHUNKS):
            result(r, n).wait()
            result_here(r, n).wait()


def body(fwd_in, fwd_routes, fwd_weights, bwd_saved, bwd_grad, bwd_routes, bwd_weights,
         expert_gate, expert_up, expert_down):
    tokens, width = fwd_in.shape[1:]
    hidden = expert_gate.shape[3]
    packed = (ROWS, width + width // 4)
    half = (2, tokens // 2, width)
    vm = pl.BlockSpec(memory_space=pltpu.VMEM)
    hbm = pl.BlockSpec(memory_space=pl.ANY)
    dma = pltpu.SemaphoreType.DMA
    shape = jax.ShapeDtypeStruct((tokens, width), BF16)
    out_f, out_b = pl.pallas_call(
        kernel,
        name="experts",
        out_shape=(shape, shape),
        in_specs=[vm] * 5 + [hbm] * 5,
        out_specs=(hbm, hbm),
        scratch_shapes=[
            pltpu.VMEM((3,) + packed, BF16), pltpu.VMEM((3,) + packed, BF16),
            pltpu.VMEM((ALL, width), BF16),
            pltpu.VMEM((2, 2, width, hidden), BF16), pltpu.VMEM((2, hidden, width), BF16),
            pltpu.VMEM((ALL, 4 * hidden), F32), pltpu.VMEM((ALL, 2 * hidden), F32),
            pltpu.VMEM((ALL, 2 * hidden), BF16), pltpu.VMEM((ALL, 2 * hidden), BF16),
            pltpu.VMEM((ALL, 2 * hidden), BF16),
            pltpu.VMEM((2,) + packed, BF16), pltpu.VMEM((2,) + packed, BF16),
            pltpu.VMEM((2, 5, 2 * tokens, ROWS), BF16),
            pltpu.VMEM(half, F32)] + [pltpu.VMEM(half, BF16)] * 5 + [
            pltpu.VMEM((2, tokens, width), BF16),
            dma((3, BLOCKS)), dma((3, BLOCKS)), dma((3,)), dma((3,)), dma((3,)),
            dma((2,)), dma((2,)), dma((2,)), dma((2,)),
            dma((2, CHUNKS, BLOCKS)), dma((2, CHUNKS, BLOCKS)), dma((2, CHUNKS)),
            dma((2, CHUNKS)), dma((2, CHUNKS)), dma((2, CHUNKS)), dma((2, CHUNKS)),
            dma((2, CHUNKS)), dma((2, CHUNKS)), dma((2, CHUNKS)), dma((3,))],
        compiler_params=pltpu.CompilerParams(
            collective_id=0, has_side_effects=True, vmem_limit_bytes=VMEM_LIMIT),
    )(fwd_routes[0].T, bwd_routes[0].T, fwd_weights[0].T, bwd_weights[0].T, bwd_saved[0], bwd_grad[0], fwd_in[0],
      expert_gate[0, 0], expert_up[0, 0], expert_down[0, 0])
    return out_f[None], out_b[None]


def solution(mesh):
    rows = P("pipe", "expert", None)
    wide = P("pipe", "expert", None, "dp")
    return jax.shard_map(
        body,
        mesh=mesh,
        in_specs=(rows,) * 7 + (wide, wide, P("pipe", "expert", "dp", None)),
        out_specs=(rows, rows),
        check_vma=False,
    )
```

```python
import jax
import jax.numpy as jnp
from jax import lax
from jax.experimental import pallas as pl
from jax.experimental.pallas import tpu as pltpu
from jax.sharding import PartitionSpec as P

MESH = pl.DeviceIdType.MESH
BF16 = jnp.bfloat16
F32 = jnp.float32

BLOCKS = 8
STEP_Z = (0, 0, 1, 1, 2, -2, -1, -1)
FAR_FIRST = (4, 5, 2, 3, 6, 7, 1, 0)
CODE = 32
ROWS = BLOCKS * 16
SPARE = BLOCKS * 4
ALL = ROWS + SPARE
VMEM_LIMIT = 56 * 1024 * 1024
SECTION = (0, -1, 1)
GROUP = 512
FOLD = GROUP // 4
WIDE = GROUP + FOLD
CHUNKS = 2
B, F = 0, 1


def place():
    pipe = lax.axis_index("pipe")
    expert = lax.axis_index("expert")
    dp = lax.axis_index("dp")
    return pipe, (dp // 2) * 4 + expert // 4, expert % 4, dp % 2


def step_x(k, core):
    return 2 * (k % 2) + (k // 2 + core) % 2


def device_of(pipe, ring, x, core):
    ring = (ring + 16) % 8
    x = (x + 8) % 4
    return ((pipe + 4) % 4, (ring % 4) * 4 + x, (ring // 4) * 2 + core)


def target_of(k):
    pipe, ring, x, core = place()
    return device_of(pipe, ring + STEP_Z[k], x + step_x(k, core), core)


def source_of(k):
    pipe, ring, x, core = place()
    return device_of(pipe, ring - STEP_Z[k], x - step_x(k, core), core)


def expert_of_block(b):
    _, ring, x, core = place()
    away = b >> 1
    return (((ring + away) & 3) << 2) + ((x + ((b & 1) << 1) + ((away + core) & 1)) & 3)


def dot(a, b):
    return jnp.dot(a, b, preferred_element_type=F32)


def dot_nt(a, b):
    return lax.dot_general(a, b, (((1,), (1,)), ((), ())), preferred_element_type=F32)


def iota(shape, dim):
    return lax.broadcasted_iota(jnp.int32, shape, dim)


def kernel(routes_f, routes_b, weights_f, weights_b, x_ref, g_ref, f_ref, gate, up, down,
           out_f, out_b,
           send, got, left, tall, tall_down, pre, back, hid, dgate, dup,
           part, home, comb, mine, other, from_other, summed, relay, from_far, final, moved,
           send_sem, recv_sem, wlocal, wsend, wrecv, shift_send, shift_recv, pass_send, pass_recv,
           rsend, rrecv, rlocal, csend, crecv, zsend, zrecv, osend, orecv, olocal, local_sem):
    pipe, ring, x, core = place()
    sibling = device_of(pipe, ring, x, 1 - core)
    up_two = device_of(pipe, ring + 2, x, core)
    down_two = device_of(pipe, ring - 2, x, core)
    after = device_of(pipe + 1, ring, x, core)
    before = device_of(pipe - 1, ring, x, core)
    tokens, width = x_ref.shape
    quarter = width // 4
    groups = width // GROUP
    cuts = [0, 5, groups]
    hidden = gate.shape[1]
    barrier = pltpu.get_barrier_semaphore()

    def greet(who):
        pl.semaphore_signal(barrier, inc=1, device_id=who, device_id_type=MESH)

    def unless_self(k, does, instead=None):
        if k:
            does()
            return
        pl.when(core == 1)(does)
        if instead is not None:
            pl.when(core == 0)(instead)

    for who in (sibling, up_two, down_two, after, before):
        greet(who)
    for k in range(BLOCKS):
        unless_self(k, lambda: greet(source_of(k)))
        unless_self(k, lambda: greet(target_of(k)))

    def here(i):
        src = (gate, up, down)[i]
        dst = tall_down.at[core] if i == 2 else tall.at[core, i]
        return pltpu.make_async_copy(src, dst, wlocal.at[i])

    def weight(i):
        src = (gate, up, down)[i]
        dst = tall_down.at[core] if i == 2 else tall.at[core, i]
        return pltpu.make_async_remote_copy(
            src_ref=src, dst_ref=dst, send_sem=wsend.at[i], recv_sem=wrecv.at[i],
            device_id=sibling, device_id_type=MESH)

    for i in range(3):
        here(i).start()

    sub, lane = iota((tokens, tokens), 0), iota((tokens, tokens), 1)

    def as_col(row):
        return jnp.sum(jnp.where(sub == lane, row, 0.0), axis=1, keepdims=True)

    def count(flags):
        return jnp.sum(jnp.where(flags, 1.0, 0.0), axis=0, keepdims=True)

    def code_rows(routes):
        r0, r1 = routes[0:1, :].astype(F32), routes[1:2, :].astype(F32)
        c0, c1 = as_col(r0), as_col(r1)
        rank0 = count((c0 == r0) & (sub < lane))
        rank1 = count(c0 == r1) + count((c1 == r1) & (sub < lane))
        return r0 * CODE + rank0, r1 * CODE + rank1

    half = tokens // 2
    my_half = pl.ds(pl.multiple_of(core * half, half), half)

    def shift(t):
        return pltpu.make_async_remote_copy(
            src_ref=(None, g_ref, f_ref)[t].at[my_half], dst_ref=moved.at[t - 1, my_half],
            send_sem=shift_send.at[t - 1], recv_sem=shift_recv.at[t - 1],
            device_id=(None, before, after)[t], device_id_type=MESH)

    def pass_on(t):
        return pltpu.make_async_remote_copy(
            src_ref=moved.at[t - 1, my_half], dst_ref=moved.at[t - 1, my_half],
            send_sem=pass_send.at[t - 1], recv_sem=pass_recv.at[t - 1],
            device_id=sibling, device_id_type=MESH)

    def blocks_of(index):
        expert = expert_of_block(index >> 4) * CODE
        return (expert + (index & 15)).astype(F32), (expert + 16 + (index & 3)).astype(F32), (index >> 2) & 3

    near_col, over_col, part_col = blocks_of(iota((ROWS, 1), 0))

    def build(t, code, rows_ref):
        first, second = code
        pick = jnp.where((first == near_col) | (second == near_col), 1.0, 0.0).astype(BF16)
        extra = jnp.where((first == over_col) | (second == over_col), 1.0, 0.0)
        total = jnp.zeros((ROWS, quarter), F32)
        for q in range(4):
            piece = rows_ref[:, q * quarter:(q + 1) * quarter]
            send[t, :, q * quarter:(q + 1) * quarter] = dot(pick, piece).astype(BF16)
            total = total + dot(jnp.where(part_col == q, extra, 0.0).astype(BF16), piece)
        send[t, :, width:] = total.astype(BF16)

    def outward(t, k):
        block = pl.ds(16 * k, 16)
        return pltpu.make_async_remote_copy(
            src_ref=send.at[t, block], dst_ref=got.at[t, block],
            send_sem=send_sem.at[t, k], recv_sem=recv_sem.at[t, k],
            device_id=target_of(k), device_id_type=MESH)

    def own_outward(t):
        return pltpu.make_async_copy(send.at[t, pl.ds(0, 16)], got.at[t, pl.ds(0, 16)], local_sem.at[t])

    def send_out(t):
        for k in FAR_FIRST:
            unless_self(k, lambda: outward(t, k).start(), lambda: own_outward(t).start())

    def wait_out(t):
        for k in FAR_FIRST:
            unless_self(k, lambda: outward(t, k).wait(), lambda: own_outward(t).wait())

    codes = [code_rows(routes) for routes in (routes_b, routes_f)]
    build(0, codes[B], x_ref)
    pl.semaphore_wait(barrier, 2 * BLOCKS + 3 + 2 * core)
    shift(1).start()
    shift(2).start()
    send_out(0)
    for i in range(3):
        weight(i).start()
    for t in (1, 2):
        shift(t).wait()
        pass_on(t).start()
    for t in (1, 2):
        pass_on(t).wait()
        build(t, codes[t - 1], moved.at[t - 1])
        send_out(t)

    near_row, over_row, part_row = blocks_of(iota((1, ROWS), 1))
    for r, weights in enumerate((weights_b, weights_f)):
        w0, w1 = as_col(weights[0:1, :]), as_col(weights[1:2, :])
        first, second = as_col(codes[r][0]), as_col(codes[r][1])
        pick = jnp.where(first == near_row, w0, 0.0) + jnp.where(second == near_row, w1, 0.0)
        extra = jnp.where(first == over_row, w0, 0.0) + jnp.where(second == over_row, w1, 0.0)
        for j in range(5):
            value = pick if j == 0 else jnp.where(part_row == j - 1, extra, 0.0)
            high = value.astype(BF16)
            comb[r, j, :tokens, :] = high
            comb[r, j, tokens:, :] = (value - high.astype(F32)).astype(BF16)

    a, b = iota((SPARE, ROWS), 0), iota((SPARE, ROWS), 1)
    fits = ((a >> 2) == (b >> 4)) & ((a & 3) == (b & 3))
    at, bt = iota((ROWS, SPARE), 0), iota((ROWS, SPARE), 1)
    fits_t = ((bt >> 2) == (at >> 4)) & ((bt & 3) == (at & 3))

    def columns(q):
        return pl.ds(pl.multiple_of(q * quarter, quarter), quarter)

    def unpack(t):
        def step(q, _):
            pick = jnp.where(fits & (((b >> 2) & 3) == q), 1.0, 0.0).astype(BF16)
            left[:ROWS, columns(q)] = got[t, :, columns(q)]
            left[ROWS:, columns(q)] = dot(pick, got[t, :, width:]).astype(BF16)
            return 0
        lax.fori_loop(0, 4, step, 0)

    def first_layer():
        pre[...] = jnp.zeros_like(pre)

        def step(q, _):
            piece = left[:, columns(q)]
            for c in range(2):
                for i in range(2):
                    lo = (2 * i + c) * hidden
                    pre[:, lo:lo + hidden] += dot(piece, tall[c, i, columns(q), :])
            return 0
        lax.fori_loop(0, 4, step, 0)

    def back_layer():
        back[...] = jnp.zeros_like(back)

        def step(q, _):
            piece = left[:, columns(q)]
            for c in range(2):
                back[:, c * hidden:(c + 1) * hidden] += dot_nt(piece, tall_down[c, :, columns(q)])
            return 0
        lax.fori_loop(0, 4, step, 0)

    packs = [jnp.where(fits_t & (((at >> 2) & 3) == q), 1.0, 0.0).astype(BF16) for q in range(4)]

    def group_cols(g, start=0, size=GROUP, pitch=GROUP):
        return pl.ds(pl.multiple_of(g * pitch + start, FOLD), size)

    def second_layer(r, n, product):
        def step(g, _):
            value = product(group_cols(g)).astype(BF16)
            part[r, :, group_cols(g, 0, GROUP, WIDE)] = value[:ROWS]
            rest = value[ROWS:]
            folded = dot(packs[0], rest[:, :FOLD])
            for q in range(1, 4):
                folded = folded + dot(packs[q], rest[:, q * FOLD:(q + 1) * FOLD])
            part[r, :, group_cols(g, GROUP, FOLD, WIDE)] = folded.astype(BF16)
            return 0
        lax.fori_loop(cuts[n], cuts[n + 1], step, 0)

    def forward_product(span):
        return dot(hid[:, :hidden], tall_down[0, :, span]) + dot(hid[:, hidden:], tall_down[1, :, span])

    def backward_product(span):
        total = dot_nt(dgate[:, :hidden], tall[0, 0, span, :])
        total = total + dot_nt(dgate[:, hidden:], tall[1, 0, span, :])
        total = total + dot_nt(dup[:, :hidden], tall[0, 1, span, :])
        return total + dot_nt(dup[:, hidden:], tall[1, 1, span, :])

    def packed_cols(n):
        return pl.ds(cuts[n] * WIDE, (cuts[n + 1] - cuts[n]) * WIDE)

    def homeward(r, n, k):
        block = pl.ds(16 * k, 16)
        return pltpu.make_async_remote_copy(
            src_ref=part.at[r, block, packed_cols(n)], dst_ref=home.at[r, block, packed_cols(n)],
            send_sem=rsend.at[r, n, k], recv_sem=rrecv.at[r, n, k],
            device_id=source_of(k), device_id_type=MESH)

    def own_homeward(r, n):
        block = pl.ds(0, 16)
        return pltpu.make_async_copy(
            part.at[r, block, packed_cols(n)], home.at[r, block, packed_cols(n)], rlocal.at[r, n])

    def send_home(r, n):
        for k in FAR_FIRST:
            unless_self(k, lambda: homeward(r, n, k).start(), lambda: own_homeward(r, n).start())

    def wait_home(r, n):
        for k in FAR_FIRST:
            unless_self(k, lambda: homeward(r, n, k).wait(), lambda: own_homeward(r, n).wait())

    for i in range(3):
        here(i).wait()
        weight(i).wait()
    wait_out(0)
    unpack(0)
    first_layer()
    wait_out(1)
    unpack(1)
    back_layer()
    pre_a = pre[:, :2 * hidden]
    sig = jax.nn.sigmoid(pre_a)
    bk = back[...]
    dgate[...] = (bk * pre[:, 2 * hidden:] * sig * (1.0 + pre_a * (1.0 - sig))).astype(BF16)
    dup[...] = (bk * pre_a * sig).astype(BF16)
    for n in range(CHUNKS):
        second_layer(B, n, backward_product)
        send_home(B, n)
    wait_out(2)
    unpack(2)
    first_layer()
    pre_a = pre[:, :2 * hidden]
    hid[...] = (pre_a * jax.nn.sigmoid(pre_a) * pre[:, 2 * hidden:]).astype(BF16)
    for n in range(CHUNKS):
        second_layer(F, n, forward_product)
        send_home(F, n)

    def span_of(n):
        return pl.ds(cuts[n] * GROUP, (cuts[n + 1] - cuts[n]) * GROUP)

    def half_of(which):
        return pl.multiple_of(which * half, half)

    def across(r, n):
        return pltpu.make_async_remote_copy(
            src_ref=other.at[r, :, span_of(n)], dst_ref=from_other.at[r, :, span_of(n)],
            send_sem=csend.at[r, n], recv_sem=crecv.at[r, n], device_id=sibling, device_id_type=MESH)

    def leg(r, n, way, first):
        rows = pl.ds(way * half // 2, half // 2)
        src, dst = (summed, relay) if first else (relay, from_far)
        stage = 0 if first else 1
        return pltpu.make_async_remote_copy(
            src_ref=src.at[r, rows, span_of(n)], dst_ref=dst.at[r, rows, span_of(n)],
            send_sem=zsend.at[stage, r, n, way], recv_sem=zrecv.at[stage, r, n, way],
            device_id=(up_two, down_two)[way], device_id_type=MESH)

    def start_along(r, n):
        for way in range(2):
            leg(r, n, way, True).start()

    def pass_along(r, n):
        for way in range(2):
            leg(r, n, way, True).wait()
            leg(r, n, way, False).start()

    def wait_along(r, n):
        for way in range(2):
            leg(r, n, way, False).wait()

    def my_result(r, n):
        return (out_b, out_f)[r].at[pl.ds(half_of(core), half), span_of(n)]

    def result(r, n):
        return pltpu.make_async_remote_copy(
            src_ref=final.at[r, :, span_of(n)], dst_ref=my_result(r, n),
            send_sem=osend.at[r, n], recv_sem=orecv.at[r, n], device_id=sibling, device_id_type=MESH)

    def result_here(r, n):
        return pltpu.make_async_copy(final.at[r, :, span_of(n)], my_result(r, n), olocal.at[r, n])

    def combine(r, n, which, dst):
        def rows_of(j):
            start = half_of(which)
            return jnp.concatenate([comb[r, j, pl.ds(start, half), :],
                                    comb[r, j, pl.ds(tokens + start, half), :]], axis=0)
        mats = [rows_of(j) for j in range(5)]

        def step(g, _):
            folded = home[r, :, group_cols(g, GROUP, FOLD, WIDE)]
            both = dot(mats[0], home[r, :, group_cols(g, 0, GROUP, WIDE)])
            both = both + jnp.concatenate([dot(m, folded) for m in mats[1:]], axis=1)
            dst[r, :, group_cols(g)] = (both[:half] + both[half:]).astype(dst.dtype)
            return 0
        lax.fori_loop(cuts[n], cuts[n + 1], step, 0)

    def gather(r, n):
        wait_home(r, n)
        combine(r, n, 1 - core, other)
        across(r, n).start()
        combine(r, n, core, mine)
        span = span_of(n)
        across(r, n).wait()
        summed[r, :, span] = (mine[r, :, span] + from_other[r, :, span].astype(F32)).astype(BF16)

    def finish(r, n):
        span = span_of(n)
        wait_along(r, n)
        final[r, :, span] = (summed[r, :, span].astype(F32) + from_far[r, :, span].astype(F32)).astype(BF16)
        result(r, n).start()
        result_here(r, n).start()

    order = [(r, n) for r in (B, F) for n in range(CHUNKS)]
    for i, piece in enumerate(order):
        gather(*piece)
        start_along(*piece)
        if i >= 1:
            pass_along(*order[i - 1])
    pass_along(*order[-1])
    for piece in order:
        finish(*piece)
    for piece in order:
        result(*piece).wait()
        result_here(*piece).wait()


def place_kernel(a, b, out_a, out_b, hold, sem):
    half = hold.shape[1] // 2
    pieces = [(i, pl.ds(h * half, half), src, dst) for i, (src, dst) in enumerate(((a, out_a), (b, out_b))) for h in range(2)]
    reads = [pltpu.make_async_copy(src.at[rows], hold.at[i, rows], sem.at[0, n])
             for n, (i, rows, src, dst) in enumerate(pieces)]
    writes = [pltpu.make_async_copy(hold.at[i, rows], dst.at[rows], sem.at[1, n])
              for n, (i, rows, src, dst) in enumerate(pieces)]
    for read in reads:
        read.start()
    for read, write in zip(reads, writes):
        read.wait()
        write.start()
    for write in writes:
        write.wait()


def body(fwd_in, fwd_routes, fwd_weights, bwd_saved, bwd_grad, bwd_routes, bwd_weights,
         expert_gate, expert_up, expert_down):
    tokens, width = fwd_in.shape[1:]
    hidden = expert_gate.shape[3]
    packed = (ROWS, width + width // 4)
    half = (2, tokens // 2, width)
    vm = pl.BlockSpec(memory_space=pltpu.VMEM)
    hbm = pl.BlockSpec(memory_space=pl.ANY)
    dma = pltpu.SemaphoreType.DMA
    shape = jax.ShapeDtypeStruct((tokens, width), BF16)
    out_f, out_b = pl.pallas_call(
        kernel,
        name="experts",
        out_shape=(shape, shape),
        in_specs=[vm] * 5 + [hbm] * 5,
        out_specs=(hbm, hbm),
        scratch_shapes=[
            pltpu.VMEM((3,) + packed, BF16), pltpu.VMEM((3,) + packed, BF16),
            pltpu.VMEM((ALL, width), BF16),
            pltpu.VMEM((2, 2, width, hidden), BF16), pltpu.VMEM((2, hidden, width), BF16),
            pltpu.VMEM((ALL, 4 * hidden), F32), pltpu.VMEM((ALL, 2 * hidden), F32),
            pltpu.VMEM((ALL, 2 * hidden), BF16), pltpu.VMEM((ALL, 2 * hidden), BF16),
            pltpu.VMEM((ALL, 2 * hidden), BF16),
            pltpu.VMEM((2,) + packed, BF16), pltpu.VMEM((2,) + packed, BF16),
            pltpu.VMEM((2, 5, 2 * tokens, ROWS), BF16),
            pltpu.VMEM(half, F32)] + [pltpu.VMEM(half, BF16)] * 6 + [
            pltpu.VMEM((2, tokens, width), BF16),
            dma((3, BLOCKS)), dma((3, BLOCKS)), dma((3,)), dma((3,)), dma((3,)),
            dma((2,)), dma((2,)), dma((2,)), dma((2,)),
            dma((2, CHUNKS, BLOCKS)), dma((2, CHUNKS, BLOCKS)), dma((2, CHUNKS)),
            dma((2, CHUNKS)), dma((2, CHUNKS)), dma((2, 2, CHUNKS, 2)), dma((2, 2, CHUNKS, 2)),
            dma((2, CHUNKS)), dma((2, CHUNKS)), dma((2, CHUNKS)), dma((3,))],
        compiler_params=pltpu.CompilerParams(
            collective_id=0, has_side_effects=True, vmem_limit_bytes=VMEM_LIMIT),
    )(fwd_routes[0].T, bwd_routes[0].T, fwd_weights[0].T, bwd_weights[0].T, bwd_saved[0], bwd_grad[0], fwd_in[0],
      expert_gate[0, 0], expert_up[0, 0], expert_down[0, 0])
    out_f, out_b = pl.pallas_call(
        place_kernel,
        name="place",
        out_shape=(shape, shape),
        in_specs=[hbm, hbm],
        out_specs=(hbm, hbm),
        scratch_shapes=[pltpu.VMEM((2, tokens, width), BF16), dma((2, 4))],
    )(out_f, out_b)
    return out_f[None], out_b[None]


def solution(mesh):
    rows = P("pipe", "expert", None)
    wide = P("pipe", "expert", None, "dp")
    return jax.shard_map(
        body,
        mesh=mesh,
        in_specs=(rows,) * 7 + (wide, wide, P("pipe", "expert", "dp", None)),
        out_specs=(rows, rows),
        check_vma=False,
    )
```

```python
import jax
import jax.numpy as jnp
from jax import lax
from jax.experimental import pallas as pl
from jax.experimental.pallas import tpu as pltpu
from jax.sharding import PartitionSpec as P

MESH = pl.DeviceIdType.MESH
BF16 = jnp.bfloat16
F32 = jnp.float32

BLOCKS = 8
STEP_Z = (0, 0, 1, 1, 2, -2, -1, -1)
FAR_FIRST = (4, 5, 2, 3, 6, 7, 1, 0)
CODE = 32
ROWS = BLOCKS * 16
SPARE = BLOCKS * 4
ALL = ROWS + SPARE
VMEM_LIMIT = 56 * 1024 * 1024
SECTION = (0, -1, 1)
GROUP = 512
FOLD = GROUP // 4
WIDE = GROUP + FOLD
CHUNKS = 2
B, F = 0, 1


def place():
    pipe = lax.axis_index("pipe")
    expert = lax.axis_index("expert")
    dp = lax.axis_index("dp")
    return pipe, (dp // 2) * 4 + expert // 4, expert % 4, dp % 2


def step_x(k, core):
    return 2 * (k % 2) + (k // 2 + core) % 2


def device_of(pipe, ring, x, core):
    ring = (ring + 16) % 8
    x = (x + 8) % 4
    return ((pipe + 4) % 4, (ring % 4) * 4 + x, (ring // 4) * 2 + core)


def target_of(k):
    pipe, ring, x, core = place()
    return device_of(pipe, ring + STEP_Z[k], x + step_x(k, core), core)


def source_of(k):
    pipe, ring, x, core = place()
    return device_of(pipe, ring - STEP_Z[k], x - step_x(k, core), core)


def expert_of_block(b):
    _, ring, x, core = place()
    away = b >> 1
    return (((ring + away) & 3) << 2) + ((x + ((b & 1) << 1) + ((away + core) & 1)) & 3)


def dot(a, b):
    return jnp.dot(a, b, preferred_element_type=F32)


def dot_nt(a, b):
    return lax.dot_general(a, b, (((1,), (1,)), ((), ())), preferred_element_type=F32)


def iota(shape, dim):
    return lax.broadcasted_iota(jnp.int32, shape, dim)


def kernel(routes_f, routes_b, weights_f, weights_b, x_ref, g_ref, f_ref, gate, up, down,
           out_f, out_b,
           send, got, left, tall, tall_down, pre, back, hid, dgate, dup,
           part, home, comb, mine, other, from_other, summed, relay, from_far, final, moved,
           send_sem, recv_sem, wlocal, wsend, wrecv, shift_send, shift_recv, pass_send, pass_recv,
           rsend, rrecv, rlocal, csend, crecv, zsend, zrecv, osend, orecv, olocal, local_sem):
    pipe, ring, x, core = place()
    sibling = device_of(pipe, ring, x, 1 - core)
    onward = device_of(pipe, ring + 2 - 4 * core, x, core)
    behind = device_of(pipe, ring - 2 + 4 * core, x, core)
    after = device_of(pipe + 1, ring, x, core)
    before = device_of(pipe - 1, ring, x, core)
    tokens, width = x_ref.shape
    quarter = width // 4
    groups = width // GROUP
    cuts = [0, 4, groups]
    hidden = gate.shape[1]
    barrier = pltpu.get_barrier_semaphore()

    def greet(who):
        pl.semaphore_signal(barrier, inc=1, device_id=who, device_id_type=MESH)

    def unless_self(k, does, instead=None):
        if k:
            does()
            return
        pl.when(core == 1)(does)
        if instead is not None:
            pl.when(core == 0)(instead)

    for who in (sibling, behind, after, before):
        greet(who)
    for k in range(BLOCKS):
        unless_self(k, lambda: greet(source_of(k)))
        unless_self(k, lambda: greet(target_of(k)))

    def here(i):
        src = (gate, up, down)[i]
        dst = tall_down.at[core] if i == 2 else tall.at[core, i]
        return pltpu.make_async_copy(src, dst, wlocal.at[i])

    def weight(i):
        src = (gate, up, down)[i]
        dst = tall_down.at[core] if i == 2 else tall.at[core, i]
        return pltpu.make_async_remote_copy(
            src_ref=src, dst_ref=dst, send_sem=wsend.at[i], recv_sem=wrecv.at[i],
            device_id=sibling, device_id_type=MESH)

    for i in range(3):
        here(i).start()

    sub, lane = iota((tokens, tokens), 0), iota((tokens, tokens), 1)

    def as_col(row):
        return jnp.sum(jnp.where(sub == lane, row, 0.0), axis=1, keepdims=True)

    def count(flags):
        return jnp.sum(jnp.where(flags, 1.0, 0.0), axis=0, keepdims=True)

    def code_rows(routes):
        r0, r1 = routes[0:1, :].astype(F32), routes[1:2, :].astype(F32)
        c0, c1 = as_col(r0), as_col(r1)
        rank0 = count((c0 == r0) & (sub < lane))
        rank1 = count(c0 == r1) + count((c1 == r1) & (sub < lane))
        return r0 * CODE + rank0, r1 * CODE + rank1

    half = tokens // 2
    my_half = pl.ds(pl.multiple_of(core * half, half), half)

    def shift(t):
        return pltpu.make_async_remote_copy(
            src_ref=(None, g_ref, f_ref)[t].at[my_half], dst_ref=moved.at[t - 1, my_half],
            send_sem=shift_send.at[t - 1], recv_sem=shift_recv.at[t - 1],
            device_id=(None, before, after)[t], device_id_type=MESH)

    def pass_on(t):
        return pltpu.make_async_remote_copy(
            src_ref=moved.at[t - 1, my_half], dst_ref=moved.at[t - 1, my_half],
            send_sem=pass_send.at[t - 1], recv_sem=pass_recv.at[t - 1],
            device_id=sibling, device_id_type=MESH)

    def blocks_of(index):
        expert = expert_of_block(index >> 4) * CODE
        return (expert + (index & 15)).astype(F32), (expert + 16 + (index & 3)).astype(F32), (index >> 2) & 3

    near_col, over_col, part_col = blocks_of(iota((ROWS, 1), 0))

    def build(t, code, rows_ref):
        first, second = code
        pick = jnp.where((first == near_col) | (second == near_col), 1.0, 0.0).astype(BF16)
        extra = jnp.where((first == over_col) | (second == over_col), 1.0, 0.0)
        total = jnp.zeros((ROWS, quarter), F32)
        for q in range(4):
            piece = rows_ref[:, q * quarter:(q + 1) * quarter]
            send[t, :, q * quarter:(q + 1) * quarter] = dot(pick, piece).astype(BF16)
            total = total + dot(jnp.where(part_col == q, extra, 0.0).astype(BF16), piece)
        send[t, :, width:] = total.astype(BF16)

    def outward(t, k):
        block = pl.ds(16 * k, 16)
        return pltpu.make_async_remote_copy(
            src_ref=send.at[t, block], dst_ref=got.at[t, block],
            send_sem=send_sem.at[t, k], recv_sem=recv_sem.at[t, k],
            device_id=target_of(k), device_id_type=MESH)

    def own_outward(t):
        return pltpu.make_async_copy(send.at[t, pl.ds(0, 16)], got.at[t, pl.ds(0, 16)], local_sem.at[t])

    def send_out(t):
        for k in FAR_FIRST:
            unless_self(k, lambda: outward(t, k).start(), lambda: own_outward(t).start())

    def wait_out(t):
        for k in FAR_FIRST:
            unless_self(k, lambda: outward(t, k).wait(), lambda: own_outward(t).wait())

    codes = [code_rows(routes) for routes in (routes_b, routes_f)]
    build(0, codes[B], x_ref)
    pl.semaphore_wait(barrier, 2 * BLOCKS + 2 + 2 * core)
    shift(1).start()
    shift(2).start()
    send_out(0)
    for i in range(3):
        weight(i).start()
    for t in (1, 2):
        shift(t).wait()
        pass_on(t).start()
    for t in (1, 2):
        pass_on(t).wait()
        build(t, codes[t - 1], moved.at[t - 1])
        send_out(t)

    near_row, over_row, part_row = blocks_of(iota((1, ROWS), 1))
    for r, weights in enumerate((weights_b, weights_f)):
        w0, w1 = as_col(weights[0:1, :]), as_col(weights[1:2, :])
        first, second = as_col(codes[r][0]), as_col(codes[r][1])
        pick = jnp.where(first == near_row, w0, 0.0) + jnp.where(second == near_row, w1, 0.0)
        extra = jnp.where(first == over_row, w0, 0.0) + jnp.where(second == over_row, w1, 0.0)
        for j in range(5):
            value = pick if j == 0 else jnp.where(part_row == j - 1, extra, 0.0)
            high = value.astype(BF16)
            comb[r, j, :tokens, :] = high
            comb[r, j, tokens:, :] = (value - high.astype(F32)).astype(BF16)

    a, b = iota((SPARE, ROWS), 0), iota((SPARE, ROWS), 1)
    fits = ((a >> 2) == (b >> 4)) & ((a & 3) == (b & 3))
    at, bt = iota((ROWS, SPARE), 0), iota((ROWS, SPARE), 1)
    fits_t = ((bt >> 2) == (at >> 4)) & ((bt & 3) == (at & 3))

    def columns(q):
        return pl.ds(pl.multiple_of(q * quarter, quarter), quarter)

    def unpack(t):
        def step(q, _):
            pick = jnp.where(fits & (((b >> 2) & 3) == q), 1.0, 0.0).astype(BF16)
            left[:ROWS, columns(q)] = got[t, :, columns(q)]
            left[ROWS:, columns(q)] = dot(pick, got[t, :, width:]).astype(BF16)
            return 0
        lax.fori_loop(0, 4, step, 0)

    def first_layer():
        pre[...] = jnp.zeros_like(pre)

        def step(q, _):
            piece = left[:, columns(q)]
            for c in range(2):
                for i in range(2):
                    lo = (2 * i + c) * hidden
                    pre[:, lo:lo + hidden] += dot(piece, tall[c, i, columns(q), :])
            return 0
        lax.fori_loop(0, 4, step, 0)

    def back_layer():
        back[...] = jnp.zeros_like(back)

        def step(q, _):
            piece = left[:, columns(q)]
            for c in range(2):
                back[:, c * hidden:(c + 1) * hidden] += dot_nt(piece, tall_down[c, :, columns(q)])
            return 0
        lax.fori_loop(0, 4, step, 0)

    packs = [jnp.where(fits_t & (((at >> 2) & 3) == q), 1.0, 0.0).astype(BF16) for q in range(4)]

    def group_cols(g, start=0, size=GROUP, pitch=GROUP):
        return pl.ds(pl.multiple_of(g * pitch + start, FOLD), size)

    def second_layer(r, n, product):
        def step(g, _):
            value = product(group_cols(g)).astype(BF16)
            part[r, :, group_cols(g, 0, GROUP, WIDE)] = value[:ROWS]
            rest = value[ROWS:]
            folded = dot(packs[0], rest[:, :FOLD])
            for q in range(1, 4):
                folded = folded + dot(packs[q], rest[:, q * FOLD:(q + 1) * FOLD])
            part[r, :, group_cols(g, GROUP, FOLD, WIDE)] = folded.astype(BF16)
            return 0
        lax.fori_loop(cuts[n], cuts[n + 1], step, 0)

    def forward_product(span):
        return dot(hid[:, :hidden], tall_down[0, :, span]) + dot(hid[:, hidden:], tall_down[1, :, span])

    def backward_product(span):
        total = dot_nt(dgate[:, :hidden], tall[0, 0, span, :])
        total = total + dot_nt(dgate[:, hidden:], tall[1, 0, span, :])
        total = total + dot_nt(dup[:, :hidden], tall[0, 1, span, :])
        return total + dot_nt(dup[:, hidden:], tall[1, 1, span, :])

    def packed_cols(n):
        return pl.ds(cuts[n] * WIDE, (cuts[n + 1] - cuts[n]) * WIDE)

    def homeward(r, n, k):
        block = pl.ds(16 * k, 16)
        return pltpu.make_async_remote_copy(
            src_ref=part.at[r, block, packed_cols(n)], dst_ref=home.at[r, block, packed_cols(n)],
            send_sem=rsend.at[r, n, k], recv_sem=rrecv.at[r, n, k],
            device_id=source_of(k), device_id_type=MESH)

    def own_homeward(r, n):
        block = pl.ds(0, 16)
        return pltpu.make_async_copy(
            part.at[r, block, packed_cols(n)], home.at[r, block, packed_cols(n)], rlocal.at[r, n])

    def send_home(r, n):
        for k in FAR_FIRST:
            unless_self(k, lambda: homeward(r, n, k).start(), lambda: own_homeward(r, n).start())

    def wait_home(r, n):
        for k in FAR_FIRST:
            unless_self(k, lambda: homeward(r, n, k).wait(), lambda: own_homeward(r, n).wait())

    for i in range(3):
        here(i).wait()
        weight(i).wait()
    wait_out(0)
    unpack(0)
    first_layer()
    wait_out(1)
    unpack(1)
    back_layer()
    pre_a = pre[:, :2 * hidden]
    sig = jax.nn.sigmoid(pre_a)
    bk = back[...]
    dgate[...] = (bk * pre[:, 2 * hidden:] * sig * (1.0 + pre_a * (1.0 - sig))).astype(BF16)
    dup[...] = (bk * pre_a * sig).astype(BF16)
    for n in range(CHUNKS):
        second_layer(B, n, backward_product)
        send_home(B, n)
    wait_out(2)
    unpack(2)
    first_layer()
    pre_a = pre[:, :2 * hidden]
    hid[...] = (pre_a * jax.nn.sigmoid(pre_a) * pre[:, 2 * hidden:]).astype(BF16)
    for n in range(CHUNKS):
        second_layer(F, n, forward_product)
        send_home(F, n)

    def span_of(n):
        return pl.ds(cuts[n] * GROUP, (cuts[n + 1] - cuts[n]) * GROUP)

    def half_of(which):
        return pl.multiple_of(which * half, half)

    def across(r, n):
        return pltpu.make_async_remote_copy(
            src_ref=other.at[r, :, span_of(n)], dst_ref=from_other.at[r, :, span_of(n)],
            send_sem=csend.at[r, n], recv_sem=crecv.at[r, n], device_id=sibling, device_id_type=MESH)

    def leg(r, n, first):
        src, dst = (summed, relay) if first else (relay, from_far)
        stage = 0 if first else 1
        return pltpu.make_async_remote_copy(
            src_ref=src.at[r, :, span_of(n)], dst_ref=dst.at[r, :, span_of(n)],
            send_sem=zsend.at[stage, r, n], recv_sem=zrecv.at[stage, r, n],
            device_id=onward, device_id_type=MESH)

    def start_along(r, n):
        leg(r, n, True).start()

    def pass_along(r, n):
        leg(r, n, True).wait()
        leg(r, n, False).start()

    def wait_along(r, n):
        leg(r, n, False).wait()

    def my_result(r, n):
        return (out_b, out_f)[r].at[pl.ds(half_of(core), half), span_of(n)]

    def result(r, n):
        return pltpu.make_async_remote_copy(
            src_ref=final.at[r, :, span_of(n)], dst_ref=my_result(r, n),
            send_sem=osend.at[r, n], recv_sem=orecv.at[r, n], device_id=sibling, device_id_type=MESH)

    def result_here(r, n):
        return pltpu.make_async_copy(final.at[r, :, span_of(n)], my_result(r, n), olocal.at[r, n])

    def combine(r, n, which, dst):
        def rows_of(j):
            start = half_of(which)
            return jnp.concatenate([comb[r, j, pl.ds(start, half), :],
                                    comb[r, j, pl.ds(tokens + start, half), :]], axis=0)
        mats = [rows_of(j) for j in range(5)]

        def step(g, _):
            folded = home[r, :, group_cols(g, GROUP, FOLD, WIDE)]
            both = dot(mats[0], home[r, :, group_cols(g, 0, GROUP, WIDE)])
            both = both + jnp.concatenate([dot(m, folded) for m in mats[1:]], axis=1)
            dst[r, :, group_cols(g)] = (both[:half] + both[half:]).astype(dst.dtype)
            return 0
        lax.fori_loop(cuts[n], cuts[n + 1], step, 0)

    def gather(r, n):
        wait_home(r, n)
        combine(r, n, 1 - core, other)
        across(r, n).start()
        combine(r, n, core, mine)
        span = span_of(n)
        across(r, n).wait()
        summed[r, :, span] = (mine[r, :, span] + from_other[r, :, span].astype(F32)).astype(BF16)

    def finish(r, n):
        span = span_of(n)
        wait_along(r, n)
        final[r, :, span] = (summed[r, :, span].astype(F32) + from_far[r, :, span].astype(F32)).astype(BF16)
        result(r, n).start()
        result_here(r, n).start()

    order = [(r, n) for r in (B, F) for n in range(CHUNKS)]
    for r in (B, F):
        for n in range(CHUNKS):
            gather(r, n)
            start_along(r, n)
        for n in range(CHUNKS):
            pass_along(r, n)
        if r == F:
            for n in range(CHUNKS):
                finish(B, n)
    for n in range(CHUNKS):
        finish(F, n)
    for piece in order:
        result(*piece).wait()
        result_here(*piece).wait()


def place_kernel(a, b, out_a, out_b, hold, sem):
    half = hold.shape[1] // 2
    pieces = [(i, pl.ds(h * half, half), src, dst) for i, (src, dst) in enumerate(((a, out_a), (b, out_b))) for h in range(2)]
    reads = [pltpu.make_async_copy(src.at[rows], hold.at[i, rows], sem.at[0, n])
             for n, (i, rows, src, dst) in enumerate(pieces)]
    writes = [pltpu.make_async_copy(hold.at[i, rows], dst.at[rows], sem.at[1, n])
              for n, (i, rows, src, dst) in enumerate(pieces)]
    for read in reads:
        read.start()
    for read, write in zip(reads, writes):
        read.wait()
        write.start()
    for write in writes:
        write.wait()


def body(fwd_in, fwd_routes, fwd_weights, bwd_saved, bwd_grad, bwd_routes, bwd_weights,
         expert_gate, expert_up, expert_down):
    tokens, width = fwd_in.shape[1:]
    hidden = expert_gate.shape[3]
    packed = (ROWS, width + width // 4)
    half = (2, tokens // 2, width)
    vm = pl.BlockSpec(memory_space=pltpu.VMEM)
    hbm = pl.BlockSpec(memory_space=pl.ANY)
    dma = pltpu.SemaphoreType.DMA
    shape = jax.ShapeDtypeStruct((tokens, width), BF16)
    out_f, out_b = pl.pallas_call(
        kernel,
        name="experts",
        out_shape=(shape, shape),
        in_specs=[vm] * 5 + [hbm] * 5,
        out_specs=(hbm, hbm),
        scratch_shapes=[
            pltpu.VMEM((3,) + packed, BF16), pltpu.VMEM((3,) + packed, BF16),
            pltpu.VMEM((ALL, width), BF16),
            pltpu.VMEM((2, 2, width, hidden), BF16), pltpu.VMEM((2, hidden, width), BF16),
            pltpu.VMEM((ALL, 4 * hidden), F32), pltpu.VMEM((ALL, 2 * hidden), F32),
            pltpu.VMEM((ALL, 2 * hidden), BF16), pltpu.VMEM((ALL, 2 * hidden), BF16),
            pltpu.VMEM((ALL, 2 * hidden), BF16),
            pltpu.VMEM((2,) + packed, BF16), pltpu.VMEM((2,) + packed, BF16),
            pltpu.VMEM((2, 5, 2 * tokens, ROWS), BF16),
            pltpu.VMEM(half, F32)] + [pltpu.VMEM(half, BF16)] * 6 + [
            pltpu.VMEM((2, tokens, width), BF16),
            dma((3, BLOCKS)), dma((3, BLOCKS)), dma((3,)), dma((3,)), dma((3,)),
            dma((2,)), dma((2,)), dma((2,)), dma((2,)),
            dma((2, CHUNKS, BLOCKS)), dma((2, CHUNKS, BLOCKS)), dma((2, CHUNKS)),
            dma((2, CHUNKS)), dma((2, CHUNKS)), dma((2, 2, CHUNKS)), dma((2, 2, CHUNKS)),
            dma((2, CHUNKS)), dma((2, CHUNKS)), dma((2, CHUNKS)), dma((3,))],
        compiler_params=pltpu.CompilerParams(
            collective_id=0, has_side_effects=True, vmem_limit_bytes=VMEM_LIMIT),
    )(fwd_routes[0].T, bwd_routes[0].T, fwd_weights[0].T, bwd_weights[0].T, bwd_saved[0], bwd_grad[0], fwd_in[0],
      expert_gate[0, 0], expert_up[0, 0], expert_down[0, 0])
    out_f, out_b = pl.pallas_call(
        place_kernel,
        name="place",
        out_shape=(shape, shape),
        in_specs=[hbm, hbm],
        out_specs=(hbm, hbm),
        scratch_shapes=[pltpu.VMEM((2, tokens, width), BF16), dma((2, 4))],
    )(out_f, out_b)
    return out_f[None], out_b[None]


def solution(mesh):
    rows = P("pipe", "expert", None)
    wide = P("pipe", "expert", None, "dp")
    return jax.shard_map(
        body,
        mesh=mesh,
        in_specs=(rows,) * 7 + (wide, wide, P("pipe", "expert", "dp", None)),
        out_specs=(rows, rows),
        check_vma=False,
    )
```

```python
import jax
import jax.numpy as jnp
from jax import lax
from jax.experimental import pallas as pl
from jax.experimental.pallas import tpu as pltpu
from jax.sharding import PartitionSpec as P

MESH = pl.DeviceIdType.MESH
BF16 = jnp.bfloat16
F32 = jnp.float32

BLOCKS = 8
STEP_Z = (0, 0, 1, 1, 2, -2, -1, -1)
FAR_FIRST = (4, 5, 2, 6, 3, 7, 1, 0)
CODE = 32
ROWS = BLOCKS * 16
SPARE = BLOCKS * 4
ALL = ROWS + SPARE
VMEM_LIMIT = 56 * 1024 * 1024
SECTION = (0, -1, 1)
GROUP = 512
FOLD = GROUP // 4
WIDE = GROUP + FOLD
CHUNKS = 2
B, F = 0, 1


def place():
    pipe = lax.axis_index("pipe")
    expert = lax.axis_index("expert")
    dp = lax.axis_index("dp")
    return pipe, (dp // 2) * 4 + expert // 4, expert % 4, dp % 2


def step_x(k, core):
    return 2 * (k % 2) + (k // 2 + core) % 2


def device_of(pipe, ring, x, core):
    ring = (ring + 16) % 8
    x = (x + 8) % 4
    return ((pipe + 4) % 4, (ring % 4) * 4 + x, (ring // 4) * 2 + core)


def target_of(k):
    pipe, ring, x, core = place()
    return device_of(pipe, ring + STEP_Z[k] * (1 - 2 * core), x + step_x(k, core), core)


def source_of(k):
    pipe, ring, x, core = place()
    return device_of(pipe, ring - STEP_Z[k] * (1 - 2 * core), x - step_x(k, core), core)


def expert_of_block(b):
    _, ring, x, core = place()
    away = b >> 1
    return (((ring + away * (1 - 2 * core)) & 3) << 2) + ((x + ((b & 1) << 1) + ((away + core) & 1)) & 3)


def dot(a, b):
    return jnp.dot(a, b, preferred_element_type=F32)


def dot_nt(a, b):
    return lax.dot_general(a, b, (((1,), (1,)), ((), ())), preferred_element_type=F32)


def iota(shape, dim):
    return lax.broadcasted_iota(jnp.int32, shape, dim)


def kernel(routes_f, routes_b, weights_f, weights_b, x_ref, g_ref, f_ref, gate, up, down,
           out_f, out_b,
           send, got, left, tall, tall_down, pre, back, hid, dgate, dup,
           part, home, comb, mine, other, from_other, summed, relay, from_far, final, moved,
           send_sem, recv_sem, wlocal, wsend, wrecv, shift_send, shift_recv, pass_send, pass_recv,
           rsend, rrecv, rlocal, csend, crecv, zsend, zrecv, osend, orecv, olocal, local_sem):
    pipe, ring, x, core = place()
    sibling = device_of(pipe, ring, x, 1 - core)
    up_two = device_of(pipe, ring + 2, x, core)
    down_two = device_of(pipe, ring - 2, x, core)
    after = device_of(pipe + 1, ring, x, core)
    before = device_of(pipe - 1, ring, x, core)
    tokens, width = x_ref.shape
    quarter = width // 4
    groups = width // GROUP
    cuts = [0, 5, groups]
    hidden = gate.shape[1]
    barrier = pltpu.get_barrier_semaphore()

    def greet(who):
        pl.semaphore_signal(barrier, inc=1, device_id=who, device_id_type=MESH)

    def unless_self(k, does, instead=None):
        if k:
            does()
            return
        pl.when(core == 1)(does)
        if instead is not None:
            pl.when(core == 0)(instead)

    for who in (sibling, up_two, down_two, after, before):
        greet(who)
    for k in range(BLOCKS):
        unless_self(k, lambda: greet(source_of(k)))
        unless_self(k, lambda: greet(target_of(k)))

    def here(i):
        src = (gate, up, down)[i]
        dst = tall_down.at[core] if i == 2 else tall.at[core, i]
        return pltpu.make_async_copy(src, dst, wlocal.at[i])

    def weight(i):
        src = (gate, up, down)[i]
        dst = tall_down.at[core] if i == 2 else tall.at[core, i]
        return pltpu.make_async_remote_copy(
            src_ref=src, dst_ref=dst, send_sem=wsend.at[i], recv_sem=wrecv.at[i],
            device_id=sibling, device_id_type=MESH)

    for i in range(3):
        here(i).start()

    sub, lane = iota((tokens, tokens), 0), iota((tokens, tokens), 1)

    def as_col(row):
        return jnp.sum(jnp.where(sub == lane, row, 0.0), axis=1, keepdims=True)

    def count(flags):
        return jnp.sum(jnp.where(flags, 1.0, 0.0), axis=0, keepdims=True)

    def code_rows(routes):
        r0, r1 = routes[0:1, :].astype(F32), routes[1:2, :].astype(F32)
        c0, c1 = as_col(r0), as_col(r1)
        rank0 = count((c0 == r0) & (sub < lane))
        rank1 = count(c0 == r1) + count((c1 == r1) & (sub < lane))
        return r0 * CODE + rank0, r1 * CODE + rank1

    half = tokens // 2
    my_half = pl.ds(pl.multiple_of(core * half, half), half)

    def shift(t):
        return pltpu.make_async_remote_copy(
            src_ref=(None, g_ref, f_ref)[t].at[my_half], dst_ref=moved.at[t - 1, my_half],
            send_sem=shift_send.at[t - 1], recv_sem=shift_recv.at[t - 1],
            device_id=(None, before, after)[t], device_id_type=MESH)

    def pass_on(t):
        return pltpu.make_async_remote_copy(
            src_ref=moved.at[t - 1, my_half], dst_ref=moved.at[t - 1, my_half],
            send_sem=pass_send.at[t - 1], recv_sem=pass_recv.at[t - 1],
            device_id=sibling, device_id_type=MESH)

    def blocks_of(index):
        expert = expert_of_block(index >> 4) * CODE
        return (expert + (index & 15)).astype(F32), (expert + 16 + (index & 3)).astype(F32), (index >> 2) & 3

    near_col, over_col, part_col = blocks_of(iota((ROWS, 1), 0))

    def build(t, code, rows_ref):
        first, second = code
        pick = jnp.where((first == near_col) | (second == near_col), 1.0, 0.0).astype(BF16)
        extra = jnp.where((first == over_col) | (second == over_col), 1.0, 0.0)
        total = jnp.zeros((ROWS, quarter), F32)
        for q in range(4):
            piece = rows_ref[:, q * quarter:(q + 1) * quarter]
            send[t, :, q * quarter:(q + 1) * quarter] = dot(pick, piece).astype(BF16)
            total = total + dot(jnp.where(part_col == q, extra, 0.0).astype(BF16), piece)
        send[t, :, width:] = total.astype(BF16)

    def outward(t, k):
        block = pl.ds(16 * k, 16)
        return pltpu.make_async_remote_copy(
            src_ref=send.at[t, block], dst_ref=got.at[t, block],
            send_sem=send_sem.at[t, k], recv_sem=recv_sem.at[t, k],
            device_id=target_of(k), device_id_type=MESH)

    def own_outward(t):
        return pltpu.make_async_copy(send.at[t, pl.ds(0, 16)], got.at[t, pl.ds(0, 16)], local_sem.at[t])

    def send_out(t):
        for k in FAR_FIRST:
            unless_self(k, lambda: outward(t, k).start(), lambda: own_outward(t).start())

    def wait_out(t):
        for k in FAR_FIRST:
            unless_self(k, lambda: outward(t, k).wait(), lambda: own_outward(t).wait())

    codes = [code_rows(routes) for routes in (routes_b, routes_f)]
    build(0, codes[B], x_ref)
    pl.semaphore_wait(barrier, 2 * BLOCKS + 3 + 2 * core)
    shift(1).start()
    shift(2).start()
    send_out(0)
    for i in range(3):
        weight(i).start()
    for t in (1, 2):
        shift(t).wait()
        pass_on(t).start()
    for t in (1, 2):
        pass_on(t).wait()
        build(t, codes[t - 1], moved.at[t - 1])
        send_out(t)

    near_row, over_row, part_row = blocks_of(iota((1, ROWS), 1))
    for r, weights in enumerate((weights_b, weights_f)):
        w0, w1 = as_col(weights[0:1, :]), as_col(weights[1:2, :])
        first, second = as_col(codes[r][0]), as_col(codes[r][1])
        pick = jnp.where(first == near_row, w0, 0.0) + jnp.where(second == near_row, w1, 0.0)
        extra = jnp.where(first == over_row, w0, 0.0) + jnp.where(second == over_row, w1, 0.0)
        for j in range(5):
            value = pick if j == 0 else jnp.where(part_row == j - 1, extra, 0.0)
            high = value.astype(BF16)
            comb[r, j, :tokens, :] = high
            comb[r, j, tokens:, :] = (value - high.astype(F32)).astype(BF16)

    a, b = iota((SPARE, ROWS), 0), iota((SPARE, ROWS), 1)
    fits = ((a >> 2) == (b >> 4)) & ((a & 3) == (b & 3))
    at, bt = iota((ROWS, SPARE), 0), iota((ROWS, SPARE), 1)
    fits_t = ((bt >> 2) == (at >> 4)) & ((bt & 3) == (at & 3))

    def columns(q):
        return pl.ds(pl.multiple_of(q * quarter, quarter), quarter)

    def unpack(t):
        def step(q, _):
            pick = jnp.where(fits & (((b >> 2) & 3) == q), 1.0, 0.0).astype(BF16)
            left[:ROWS, columns(q)] = got[t, :, columns(q)]
            left[ROWS:, columns(q)] = dot(pick, got[t, :, width:]).astype(BF16)
            return 0
        lax.fori_loop(0, 4, step, 0)

    def first_layer():
        pre[...] = jnp.zeros_like(pre)

        def step(q, _):
            piece = left[:, columns(q)]
            for c in range(2):
                for i in range(2):
                    lo = (2 * i + c) * hidden
                    pre[:, lo:lo + hidden] += dot(piece, tall[c, i, columns(q), :])
            return 0
        lax.fori_loop(0, 4, step, 0)

    def back_layer():
        back[...] = jnp.zeros_like(back)

        def step(q, _):
            piece = left[:, columns(q)]
            for c in range(2):
                back[:, c * hidden:(c + 1) * hidden] += dot_nt(piece, tall_down[c, :, columns(q)])
            return 0
        lax.fori_loop(0, 4, step, 0)

    packs = [jnp.where(fits_t & (((at >> 2) & 3) == q), 1.0, 0.0).astype(BF16) for q in range(4)]

    def group_cols(g, start=0, size=GROUP, pitch=GROUP):
        return pl.ds(pl.multiple_of(g * pitch + start, FOLD), size)

    def second_layer(r, n, product):
        def step(g, _):
            value = product(group_cols(g)).astype(BF16)
            part[r, :, group_cols(g, 0, GROUP, WIDE)] = value[:ROWS]
            rest = value[ROWS:]
            folded = dot(packs[0], rest[:, :FOLD])
            for q in range(1, 4):
                folded = folded + dot(packs[q], rest[:, q * FOLD:(q + 1) * FOLD])
            part[r, :, group_cols(g, GROUP, FOLD, WIDE)] = folded.astype(BF16)
            return 0
        lax.fori_loop(cuts[n], cuts[n + 1], step, 0)

    def forward_product(span):
        return dot(hid[:, :hidden], tall_down[0, :, span]) + dot(hid[:, hidden:], tall_down[1, :, span])

    def backward_product(span):
        total = dot_nt(dgate[:, :hidden], tall[0, 0, span, :])
        total = total + dot_nt(dgate[:, hidden:], tall[1, 0, span, :])
        total = total + dot_nt(dup[:, :hidden], tall[0, 1, span, :])
        return total + dot_nt(dup[:, hidden:], tall[1, 1, span, :])

    def packed_cols(n):
        return pl.ds(cuts[n] * WIDE, (cuts[n + 1] - cuts[n]) * WIDE)

    def homeward(r, n, k):
        block = pl.ds(16 * k, 16)
        return pltpu.make_async_remote_copy(
            src_ref=part.at[r, block, packed_cols(n)], dst_ref=home.at[r, block, packed_cols(n)],
            send_sem=rsend.at[r, n, k], recv_sem=rrecv.at[r, n, k],
            device_id=source_of(k), device_id_type=MESH)

    def own_homeward(r, n):
        block = pl.ds(0, 16)
        return pltpu.make_async_copy(
            part.at[r, block, packed_cols(n)], home.at[r, block, packed_cols(n)], rlocal.at[r, n])

    def send_home(r, n):
        for k in FAR_FIRST:
            unless_self(k, lambda: homeward(r, n, k).start(), lambda: own_homeward(r, n).start())

    def wait_home(r, n):
        for k in FAR_FIRST:
            unless_self(k, lambda: homeward(r, n, k).wait(), lambda: own_homeward(r, n).wait())

    for i in range(3):
        here(i).wait()
        weight(i).wait()
    wait_out(0)
    unpack(0)
    first_layer()
    wait_out(1)
    unpack(1)
    back_layer()
    pre_a = pre[:, :2 * hidden]
    sig = jax.nn.sigmoid(pre_a)
    bk = back[...]
    dgate[...] = (bk * pre[:, 2 * hidden:] * sig * (1.0 + pre_a * (1.0 - sig))).astype(BF16)
    dup[...] = (bk * pre_a * sig).astype(BF16)
    for n in range(CHUNKS):
        second_layer(B, n, backward_product)
        send_home(B, n)
    wait_out(2)
    unpack(2)
    first_layer()
    pre_a = pre[:, :2 * hidden]
    hid[...] = (pre_a * jax.nn.sigmoid(pre_a) * pre[:, 2 * hidden:]).astype(BF16)
    for n in range(CHUNKS):
        second_layer(F, n, forward_product)
        send_home(F, n)

    def span_of(n):
        return pl.ds(cuts[n] * GROUP, (cuts[n + 1] - cuts[n]) * GROUP)

    def half_of(which):
        return pl.multiple_of(which * half, half)

    def across(r, n):
        return pltpu.make_async_remote_copy(
            src_ref=other.at[r, :, span_of(n)], dst_ref=from_other.at[r, :, span_of(n)],
            send_sem=csend.at[r, n], recv_sem=crecv.at[r, n], device_id=sibling, device_id_type=MESH)

    def leg(r, n, way, first):
        rows = pl.ds(way * half // 2, half // 2)
        src, dst = (summed, relay) if first else (relay, from_far)
        stage = 0 if first else 1
        return pltpu.make_async_remote_copy(
            src_ref=src.at[r, rows, span_of(n)], dst_ref=dst.at[r, rows, span_of(n)],
            send_sem=zsend.at[stage, r, n, way], recv_sem=zrecv.at[stage, r, n, way],
            device_id=(up_two, down_two)[way], device_id_type=MESH)

    def start_along(r, n):
        for way in range(2):
            leg(r, n, way, True).start()

    def pass_along(r, n):
        for way in range(2):
            leg(r, n, way, True).wait()
            leg(r, n, way, False).start()

    def wait_along(r, n):
        for way in range(2):
            leg(r, n, way, False).wait()

    def my_result(r, n):
        return (out_b, out_f)[r].at[pl.ds(half_of(core), half), span_of(n)]

    def result(r, n):
        return pltpu.make_async_remote_copy(
            src_ref=final.at[r, :, span_of(n)], dst_ref=my_result(r, n),
            send_sem=osend.at[r, n], recv_sem=orecv.at[r, n], device_id=sibling, device_id_type=MESH)

    def result_here(r, n):
        return pltpu.make_async_copy(final.at[r, :, span_of(n)], my_result(r, n), olocal.at[r, n])

    def combine(r, n, which, dst):
        def rows_of(j):
            start = half_of(which)
            return jnp.concatenate([comb[r, j, pl.ds(start, half), :],
                                    comb[r, j, pl.ds(tokens + start, half), :]], axis=0)
        mats = [rows_of(j) for j in range(5)]

        def step(g, _):
            folded = home[r, :, group_cols(g, GROUP, FOLD, WIDE)]
            both = dot(mats[0], home[r, :, group_cols(g, 0, GROUP, WIDE)])
            both = both + jnp.concatenate([dot(m, folded) for m in mats[1:]], axis=1)
            dst[r, :, group_cols(g)] = (both[:half] + both[half:]).astype(dst.dtype)
            return 0
        lax.fori_loop(cuts[n], cuts[n + 1], step, 0)

    def gather(r, n):
        wait_home(r, n)
        combine(r, n, 1 - core, other)
        across(r, n).start()
        combine(r, n, core, mine)
        span = span_of(n)
        across(r, n).wait()
        summed[r, :, span] = (mine[r, :, span] + from_other[r, :, span].astype(F32)).astype(BF16)

    def finish(r, n):
        span = span_of(n)
        wait_along(r, n)
        final[r, :, span] = (summed[r, :, span].astype(F32) + from_far[r, :, span].astype(F32)).astype(BF16)
        result(r, n).start()
        result_here(r, n).start()

    order = [(r, n) for r in (B, F) for n in range(CHUNKS)]
    for i, piece in enumerate(order):
        gather(*piece)
        start_along(*piece)
        if i >= 1:
            pass_along(*order[i - 1])
    pass_along(*order[-1])
    for piece in order:
        finish(*piece)
    for piece in order:
        result(*piece).wait()
        result_here(*piece).wait()


def place_kernel(a, b, out_a, out_b, hold, sem):
    half = hold.shape[1] // 2
    pieces = [(i, pl.ds(h * half, half), src, dst) for i, (src, dst) in enumerate(((a, out_a), (b, out_b))) for h in range(2)]
    reads = [pltpu.make_async_copy(src.at[rows], hold.at[i, rows], sem.at[0, n])
             for n, (i, rows, src, dst) in enumerate(pieces)]
    writes = [pltpu.make_async_copy(hold.at[i, rows], dst.at[rows], sem.at[1, n])
              for n, (i, rows, src, dst) in enumerate(pieces)]
    for read in reads:
        read.start()
    for read, write in zip(reads, writes):
        read.wait()
        write.start()
    for write in writes:
        write.wait()


def body(fwd_in, fwd_routes, fwd_weights, bwd_saved, bwd_grad, bwd_routes, bwd_weights,
         expert_gate, expert_up, expert_down):
    tokens, width = fwd_in.shape[1:]
    hidden = expert_gate.shape[3]
    packed = (ROWS, width + width // 4)
    half = (2, tokens // 2, width)
    vm = pl.BlockSpec(memory_space=pltpu.VMEM)
    hbm = pl.BlockSpec(memory_space=pl.ANY)
    dma = pltpu.SemaphoreType.DMA
    shape = jax.ShapeDtypeStruct((tokens, width), BF16)
    out_f, out_b = pl.pallas_call(
        kernel,
        name="experts",
        out_shape=(shape, shape),
        in_specs=[vm] * 5 + [hbm] * 5,
        out_specs=(hbm, hbm),
        scratch_shapes=[
            pltpu.VMEM((3,) + packed, BF16), pltpu.VMEM((3,) + packed, BF16),
            pltpu.VMEM((ALL, width), BF16),
            pltpu.VMEM((2, 2, width, hidden), BF16), pltpu.VMEM((2, hidden, width), BF16),
            pltpu.VMEM((ALL, 4 * hidden), F32), pltpu.VMEM((ALL, 2 * hidden), F32),
            pltpu.VMEM((ALL, 2 * hidden), BF16), pltpu.VMEM((ALL, 2 * hidden), BF16),
            pltpu.VMEM((ALL, 2 * hidden), BF16),
            pltpu.VMEM((2,) + packed, BF16), pltpu.VMEM((2,) + packed, BF16),
            pltpu.VMEM((2, 5, 2 * tokens, ROWS), BF16),
            pltpu.VMEM(half, F32)] + [pltpu.VMEM(half, BF16)] * 6 + [
            pltpu.VMEM((2, tokens, width), BF16),
            dma((3, BLOCKS)), dma((3, BLOCKS)), dma((3,)), dma((3,)), dma((3,)),
            dma((2,)), dma((2,)), dma((2,)), dma((2,)),
            dma((2, CHUNKS, BLOCKS)), dma((2, CHUNKS, BLOCKS)), dma((2, CHUNKS)),
            dma((2, CHUNKS)), dma((2, CHUNKS)), dma((2, 2, CHUNKS, 2)), dma((2, 2, CHUNKS, 2)),
            dma((2, CHUNKS)), dma((2, CHUNKS)), dma((2, CHUNKS)), dma((3,))],
        compiler_params=pltpu.CompilerParams(
            collective_id=0, has_side_effects=True, vmem_limit_bytes=VMEM_LIMIT),
    )(fwd_routes[0].T, bwd_routes[0].T, fwd_weights[0].T, bwd_weights[0].T, bwd_saved[0], bwd_grad[0], fwd_in[0],
      expert_gate[0, 0], expert_up[0, 0], expert_down[0, 0])
    out_f, out_b = pl.pallas_call(
        place_kernel,
        name="place",
        out_shape=(shape, shape),
        in_specs=[hbm, hbm],
        out_specs=(hbm, hbm),
        scratch_shapes=[pltpu.VMEM((2, tokens, width), BF16), dma((2, 4))],
    )(out_f, out_b)
    return out_f[None], out_b[None]


def solution(mesh):
    rows = P("pipe", "expert", None)
    wide = P("pipe", "expert", None, "dp")
    return jax.shard_map(
        body,
        mesh=mesh,
        in_specs=(rows,) * 7 + (wide, wide, P("pipe", "expert", "dp", None)),
        out_specs=(rows, rows),
        check_vma=False,
    )
```
